256 devices in a mesh: nest: 64 (over z, y_hi, x), parent: 4 (over y_lo, core).
Axes of the slice: x: 4, y: 4 (y_hi: 2, y_lo: 2; y = y_hi * 2 + y_lo), z: 8, core: 2. Of those that a mesh axis runs over, the one named last changes fastest.
Arguments:
- nest_state: float32 [4, 64, 64, 8192], P(None, None, 'parent', 'nest'), may hold values from -6 to 6
- mixing: float32 [64, 8192], P('parent', 'nest'), may hold values from 0.02 to 0.2
- land_mask: int32 [64, 8192], P('parent', 'nest'), may hold values 0 or 1
- face_off: int32 [64, 128], P('parent', 'nest'), may hold values from 0 to 3, as said below
- parent_state: float32 [4, 64, 4, 8192], P(None, None, 'parent', 'nest'), may hold values from -6 to 6
- parent_block: int32 [4, 64], P('parent', 'nest'), may hold values from 0 to 63, as said below
- interp_idx: int32 [64, 128, 4], P('parent', 'nest'), may hold values from 0 to 127
- interp_w: float32 [64, 128, 4], P('parent', 'nest'), may hold values from 0.1 to 1
Outputs:
- nest_new: float32 [4, 64, 64, 8192], P(None, None, 'parent', 'nest')
- parent_new: float32 [4, 64, 4, 8192], P(None, None, 'parent', 'nest')
The draws below stay inside these ranges and needn't reach their ends.
Inputs may be any that keep to these rules, and one draw needn't show every extreme that they name: `face_off`: entry 2n of a row is tile n's west face, 2n+1 its east face; d > 0 names the tile d places west (east) in the same row block, never beyond the ends; the value 3 occurs in every draw. `parent_block`: each row is a permutation of 0 to 63 that keeps every aligned group of 4 tiles, so the block lies at most 3 tiles from its nest tile; that distance is reached in every draw.
All inputs are finite; a program needn't handle non-finite values. No bound on the sum of `land_mask` on one device may be relied on, other than what follows from the above.
Results may differ from the reference program's by a relative error of at most 0.00002.
Values sent between devices are 32-bit elements; how exact they have to be, the bound alone decides.
No kernel may reach another device: no remote copies, remote signals or barrier semaphores. Data moves between devices by JAX's collectives and lax.ppermute only.
A program may use at most 128 MiB of HBM per device.

```python
import math
import jax
import jax.numpy as jnp

F = 4
LEV = 64
CY = 16
CX = 128
ITERS = 4
RADIUS = 3
RATIO = 4
TILES = 64
NY = 64
NX = 8192
PCELLS = 128
N_PARENT = 4


def draw_face_off(key, part):
    key = jax.random.fold_in(key, 11)
    subkeys = jax.random.split(key, 2)
    split_row = jax.random.randint(subkeys[0], (N_PARENT, 1, TILES, 2), 0, CY + 1)
    offset_pair = jax.random.randint(subkeys[1], (N_PARENT, 2, TILES, 2), 0, RADIUS + 1)
    row_index = jnp.arange(CY)[None, :, None, None]
    offsets = jnp.where(row_index < split_row, offset_pair[:, 0:1], offset_pair[:, 1:2])
    tile_index = jnp.arange(TILES)[None, None, :, None]
    side_index = jnp.arange(2)[None, None, None, :]
    reach_end = jnp.where(side_index == 0, tile_index, TILES - 1 - tile_index)
    offsets = jnp.where(offsets <= reach_end, offsets, 0)
    forced = (row_index == 0) & (tile_index == RADIUS) & (side_index == 0)
    offsets = jnp.where(forced, RADIUS, offsets)
    return offsets.reshape(N_PARENT * CY, TILES * 2).astype(jnp.int32)


def draw_parent_block(key, part):
    key = jax.random.fold_in(key, 23)
    group_size = RADIUS + 1
    group_count = TILES // group_size
    scores = jax.random.randint(key, (N_PARENT, group_count, group_size), 0, 1 << 20) * group_size + jnp.arange(group_size)
    shuffle = jnp.argsort(scores, axis=-1).astype(jnp.int32)
    reverse = (group_size - 1 - jnp.arange(group_size))[None, None, :]
    leading = (jnp.arange(group_count) == 0)[None, :, None]
    shuffle = jnp.where(leading, reverse, shuffle)
    starts = (jnp.arange(group_count) * group_size)[None, :, None]
    return (starts + shuffle).reshape(N_PARENT, TILES).astype(jnp.int32)


def with_ends(values, rng, low, largest):
    dims = values.shape
    spot = [jax.random.randint(jax.random.fold_in(rng, axis), (), 0, dims[axis]) for axis in range(len(dims))]
    values = values.at[tuple(spot)].set(low)
    longest = dims.index(max(dims))
    spot[longest] = (spot[longest] + 1) % dims[longest]
    return values.at[tuple(spot)].set(largest)


def steps_of(stream_key, shape, cuts, least, largest):
    factor_of, own = 1.0, jax.random.fold_in(stream_key, 6)
    for position, shards_of in cuts:
        draws = jnp.exp(jax.random.uniform(jax.random.fold_in(own, position), (shards_of,), jnp.float32, least / len(cuts), largest / len(cuts)))
        factor_of = factor_of * jnp.repeat(draws, shape[position] // shards_of).reshape([-1 if axis == position else 1 for axis in range(len(shape))])
    return factor_of


def centred(own_key, dims, spread, bound, cuts=(), kind=jnp.bfloat16):
    entries = jax.random.normal(own_key, dims, jnp.float32) * spread
    if len(cuts) > 0:
        entries = steps_of(own_key, dims, cuts, -0.22, 0.18) * entries
    return jnp.clip(entries, min=-bound, max=bound).astype(kind)


def setup_inputs(seed: int = 0) -> dict:
    key_of = jax.random.split(jax.random.key(seed), 9)
    return {
        "nest_state": centred(key_of[0], (F, LEV, NY, NX), 1.0, 6.0, ((2, 4), (3, 64)), jnp.float32),
        "mixing": jnp.clip(jnp.exp(math.log(0.2) - 2.3025851 * jax.random.uniform(key_of[1], (NY, NX), jnp.float32) ** steps_of(key_of[1], (NY, NX), ((0, 4), (1, 64)), -0.2, 0.2)), 0.02, 0.2),
        "land_mask": with_ends((jax.random.randint(key_of[2], (NY, NX), 0, 8) < 7).astype(jnp.int32), jax.random.fold_in(key_of[2], 1), 0, 1),
        "face_off": draw_face_off(jax.random.fold_in(key_of[8], 71), 0),
        "parent_state": centred(key_of[4], (F, LEV, N_PARENT, TILES * PCELLS), 1.0, 6.0, ((2, 4), (3, 64)), jnp.float32),
        "parent_block": draw_parent_block(jax.random.fold_in(key_of[8], 71), 0),
        "interp_idx": with_ends(jax.random.randint(key_of[6], (NY, 2 * TILES, 4), 0, PCELLS), jax.random.fold_in(key_of[6], 1), 0, PCELLS - 1).astype(jnp.int32),
        "interp_w": jnp.clip(0.1 + 0.9 * jax.random.uniform(key_of[7], (NY, 2 * TILES, 4), jnp.float32) ** steps_of(key_of[7], (NY, 2 * TILES, 4), ((0, 4), (1, 64)), -0.2, 0.2), 0.1, 1.0),
    }


TIME_STEP = 0.1
DIFFUSION = 1.0
CORIOLIS = 0.5
FEEDBACK = 0.5


def advance(current, padded_x, padded_y, mixing, wet_mask):
    slope_x = ((padded_x[..., 2:] - padded_x[..., :-2]) * 0.5).reshape(current.shape)
    pair_x = (padded_x[..., 2:] + padded_x[..., :-2]).reshape(current.shape)
    slope_y = (padded_y[:, :, 2:] - padded_y[:, :, :-2]) * 0.5
    pair_y = padded_y[:, :, 2:] + padded_y[:, :, :-2]
    level_above = jnp.concatenate([current[:, :1], current[:, :-1]], axis=1)
    level_below = jnp.concatenate([current[:, 1:], current[:, -1:]], axis=1)
    zonal_flow = current[2]
    merid_flow = current[3]
    tendency = -(zonal_flow * slope_x + merid_flow * slope_y) + DIFFUSION * (pair_x + pair_y - 4.0 * current)
    updated = current + TIME_STEP * tendency + mixing * (level_above + level_below - 2.0 * current)
    blank = jnp.zeros_like(zonal_flow)
    rotation = jnp.stack([blank, blank, TIME_STEP * CORIOLIS * merid_flow, -TIME_STEP * CORIOLIS * zonal_flow])
    return (updated + rotation) * wet_mask


def reference(nest_state, mixing, land_mask, face_off, parent_state, parent_block, interp_idx, interp_w):
    wet_mask = land_mask.astype(jnp.float32)
    stencil_idx = interp_idx.reshape(N_PARENT, CY, TILES, 2, 4)
    stencil_w = interp_w.reshape(N_PARENT, CY, TILES, 2, 4)
    flat_idx = (parent_block[:, None, :, None, None] * PCELLS + stencil_idx).astype(jnp.int32)
    coarse = parent_state.reshape(F, LEV, N_PARENT, TILES * PCELLS)
    index_rows = jnp.broadcast_to(flat_idx.reshape(N_PARENT, CY * TILES * 8)[None, None], (F, LEV, N_PARENT, CY * TILES * 8))
    picked = jnp.take_along_axis(coarse, index_rows, axis=3).reshape(F, LEV, N_PARENT, CY, TILES, 2, 4)
    open_vals = jnp.sum(picked * stencil_w, axis=-1) / jnp.sum(stencil_w, axis=-1)
    open_vals = open_vals.reshape(F, LEV, NY, TILES, 2)
    offsets = face_off.reshape(NY, TILES, 2)
    tile_index = jnp.arange(TILES, dtype=jnp.int32)
    west_src = jnp.clip(tile_index[None, :] - offsets[..., 0], 0, TILES - 1).astype(jnp.int32)
    east_src = jnp.clip(tile_index[None, :] + offsets[..., 1], 0, TILES - 1).astype(jnp.int32)
    edge_shape = (F, LEV, NY, TILES)
    current = nest_state
    for substep in range(ITERS):
        tile_view = current.reshape(F, LEV, NY, TILES, CX)
        from_west = jnp.take_along_axis(tile_view[..., CX - 1], jnp.broadcast_to(west_src, edge_shape), axis=3)
        from_east = jnp.take_along_axis(tile_view[..., 0], jnp.broadcast_to(east_src, edge_shape), axis=3)
        west_ghost = jnp.where(offsets[..., 0] == 0, open_vals[..., 0], from_west)
        east_ghost = jnp.where(offsets[..., 1] == 0, open_vals[..., 1], from_east)
        padded_x = jnp.concatenate([west_ghost[..., None], tile_view, east_ghost[..., None]], axis=-1)
        padded_y = jnp.pad(current, ((0, 0), (0, 0), (1, 1), (0, 0)))
        current = advance(current, padded_x, padded_y, mixing, wet_mask)
    fine_view = current.reshape(F, LEV, N_PARENT, CY // RATIO, RATIO, TILES, CX // RATIO, RATIO)
    block_means = jnp.mean(fine_view, axis=(4, 7))
    block_means = jnp.transpose(block_means, (0, 1, 2, 4, 3, 5)).reshape(F, LEV, N_PARENT, TILES, PCELLS)
    owner = jnp.zeros((N_PARENT, TILES), jnp.int32).at[jnp.arange(N_PARENT, dtype=jnp.int32)[:, None], parent_block].set(jnp.broadcast_to(tile_index[None, :], (N_PARENT, TILES)))
    received = jnp.take_along_axis(block_means, jnp.broadcast_to(owner[None, None, :, :, None], (F, LEV, N_PARENT, TILES, PCELLS)), axis=3)
    parent_tiles = parent_state.reshape(F, LEV, N_PARENT, TILES, PCELLS)
    parent_new = (parent_tiles + FEEDBACK * (received - parent_tiles)).reshape(F, LEV, N_PARENT, TILES * PCELLS)
    return current, parent_new
```

```python
import functools

import jax
import jax.numpy as jnp
from jax import lax
from jax.experimental import pallas as pl
from jax.experimental.pallas import tpu as pltpu
from jax.sharding import PartitionSpec as P

FIELDS = 4
LEVELS = 64
ROWS = 16
COLS = 128
HALO = 4
EXT = ROWS + 2 * HALO
HALF = LEVELS // 2
PLANES = 2 * FIELDS
PAD = 8
STATE_ROWS = FIELDS * LEVELS * EXT + 2 * PAD
PACK_ROWS = PLANES * EXT
SIDE_ROWS = PACK_ROWS + EXT
REACH = 3
SLOTS = 2 * REACH + 1
GROUP = 4
UNROLL = 4
VMEM_BYTES = 44 * 1024 * 1024

TIME_STEP = 0.1
TURN = 0.05
FEEDBACK = 0.5

S_EVEN, S_TOP, S_BOTTOM, S_PBX, S_SLOT, S_XEVEN, S_LOW, S_PB = 0, 1, 2, 3, 4, 10, 11, 12


def lanes():
    return lax.broadcasted_iota(jnp.int32, (8, COLS), 1)


def send_rows_kernel(sc, nest, pay1, pay2):
    even = sc[S_EVEN] == 1
    first = jnp.where(even, ROWS - HALO, 0)
    second = jnp.where(even, 0, ROWS - HALO)

    def body(i, carry):
        for j in range(8):
            at = (i * 8 + j) * ROWS
            to = (i * 8 + j) * HALO
            pay1[pl.ds(to, HALO), :] = nest[pl.ds(at + first, HALO), :]
            pay2[pl.ds(to, HALO), :] = nest[pl.ds(at + second, HALO), :]
        return carry

    lax.fori_loop(0, FIELDS * LEVELS // 8, body, 0)


def open_kernel(sc, own, got1, got2, got3, idx, weight, face, mask, mixing, og, off, pay1, pay2):
    pbx = sc[S_PBX]
    chosen = own[...]
    for code, got in ((1, got1), (2, got2), (3, got3)):
        chosen = jnp.where(pbx == code, got[...], chosen)
    cell = lax.broadcasted_iota(jnp.int32, (ROWS, COLS), 1)
    spread = []
    for side in range(2):
        total = jnp.zeros((ROWS, 1), jnp.float32)
        table = jnp.zeros((ROWS, COLS), jnp.float32)
        for j in range(4):
            w = weight[:, side * 4 + j : side * 4 + j + 1]
            total = total + w
            table = table + jnp.where(idx[:, side * 4 + j : side * 4 + j + 1] == cell, w, 0.0)
        spread.append(table / total)
    table = jnp.concatenate(spread, axis=0)
    values = lax.dot_general(
        table, chosen, (((1,), (1,)), ((), ())),
        precision=lax.Precision.HIGHEST, preferred_element_type=jnp.float32,
    )
    source = lax.broadcasted_iota(jnp.int32, (COLS, COLS), 0)
    target = lax.broadcasted_iota(jnp.int32, (COLS, COLS), 1)
    lane16 = lax.broadcasted_iota(jnp.int32, (ROWS, COLS), 1)
    column = lane16 % 4
    wcol = face[:, 0:1].astype(jnp.float32)
    ecol = face[:, 1:2].astype(jnp.float32)
    off_plane = jnp.where(column == 1, wcol, ecol)
    off[...] = off_plane
    planes = []
    for h in range(2):
        for f in range(FIELDS):
            quarter = (f % 2) * 2 + h
            expand = (source == quarter * HALF + target // 4).astype(jnp.float32)
            block = values[:, (f // 2) * COLS : (f // 2 + 1) * COLS]
            wide = lax.dot_general(
                block, expand, (((1,), (0,)), ((), ())),
                precision=lax.Precision.HIGHEST, preferred_element_type=jnp.float32,
            )
            plane = jnp.where(column == 1, wide[:ROWS], wide[ROWS:])
            og[pl.ds((h * FIELDS + f) * ROWS, ROWS), :] = plane
            planes.append(plane)
    planes += [mask[...].astype(jnp.float32), mixing[...], off_plane]
    even = sc[S_EVEN] == 1
    for i, plane in enumerate(planes):
        low, high = plane[:HALO], plane[ROWS - HALO :]
        pay1[pl.ds(i * HALO, HALO), :] = jnp.where(even, high, low)
        pay2[pl.ds(i * HALO, HALO), :] = jnp.where(even, low, high)


def pack_into(acc, value, k, lane):
    hit = (lane // 4) == k
    return jnp.where(hit, pltpu.roll(value, 4 * k + 2, 1), acc)


def extend_kernel(
    sc, nest, wide1, wide2, og, off, mask, mixing, edge1, edge2,
    ext, pack, og_ext, stat, msg_e, msg_o, msg_lo, msg_hi,
):
    even = sc[S_EVEN] == 1
    top_in = sc[S_TOP] == 1
    bottom_in = sc[S_BOTTOM] == 1

    def halos(one, two):
        top = jnp.where(top_in, jnp.where(even, two, one), 0.0)
        bottom = jnp.where(bottom_in, jnp.where(even, one, two), 0.0)
        return top, bottom

    zero_pad = jnp.zeros((PAD, COLS), jnp.float32)
    ext[pl.ds(0, PAD), :] = zero_pad
    ext[pl.ds(STATE_ROWS - PAD, PAD), :] = zero_pad

    def fill(i, carry):
        for j in range(4):
            fk = i * 4 + j
            base = PAD + fk * EXT
            top, bottom = halos(wide1[pl.ds(fk * HALO, HALO), :], wide2[pl.ds(fk * HALO, HALO), :])
            ext[pl.ds(base, HALO), :] = top
            ext[pl.ds(base + HALO, 8), :] = nest[pl.ds(fk * ROWS, 8), :]
            ext[pl.ds(base + HALO + 8, 8), :] = nest[pl.ds(fk * ROWS + 8, 8), :]
            ext[pl.ds(base + HALO + ROWS, HALO), :] = bottom
        return carry

    lax.fori_loop(0, FIELDS * LEVELS // 4, fill, 0)

    def put(dst, base, own, plane):
        top, bottom = halos(edge1[pl.ds(plane * HALO, HALO), :], edge2[pl.ds(plane * HALO, HALO), :])
        dst[pl.ds(base, HALO), :] = top
        dst[pl.ds(base + HALO, ROWS), :] = own
        dst[pl.ds(base + HALO + ROWS, HALO), :] = bottom

    for i in range(PLANES):
        put(og_ext, i * EXT, og[pl.ds(i * ROWS, ROWS), :], i)
    put(stat, 0, mask[...].astype(jnp.float32), PLANES)
    put(stat, EXT, mixing[...], PLANES + 1)
    put(stat, 2 * EXT, off[...], PLANES + 2)

    lane = lanes()
    column = lane % 4
    for g in range(3):
        for h in range(2):

            def gather(i, acc, g=g, h=h):
                acc = list(acc)
                for j in range(UNROLL):
                    k = i * UNROLL + j
                    for f in range(FIELDS):
                        at = PAD + (f * LEVELS + h * HALF + k) * EXT + 8 * g
                        acc[f] = pack_into(acc[f], ext[pl.ds(at, 8), :], k, lane)
                return tuple(acc)

            acc = lax.fori_loop(
                0, HALF // UNROLL, gather, tuple(jnp.zeros((8, COLS), jnp.float32) for _ in range(FIELDS))
            )
            for f in range(FIELDS):
                pack[pl.ds((h * FIELDS + f) * EXT + 8 * g, 8), :] = acc[f]

    x_even = sc[S_XEVEN] == 1
    low = sc[S_LOW] == 1
    number = sc[S_PB].astype(jnp.float32)
    for i in range(PLANES + 1):
        for g in range(3):
            rows = pl.ds(i * EXT + 8 * g, 8)
            if i < PLANES:
                own, opened = pack[rows, :], og_ext[rows, :]
                right = jnp.where(column == 3, pltpu.roll(opened, 1, 1), own)
                left = jnp.where(column == 0, pltpu.roll(opened, COLS - 1, 1), own)
            else:
                wet = stat[pl.ds(8 * g, 8), :]
                mix = stat[pl.ds(EXT + 8 * g, 8), :]
                away = stat[pl.ds(2 * EXT + 8 * g, 8), :]
                right = jnp.where(lane == 0, pltpu.roll(wet, 1, 1), jnp.where(lane == 1, pltpu.roll(mix, 2, 1), away))
                left = jnp.where(
                    lane == 0, wet, jnp.where(lane == 1, pltpu.roll(mix, 1, 1), pltpu.roll(away, 1, 1))
                )
                right = jnp.where(lane == 3, number, right)
                left = jnp.where(lane == 3, number, left)
            msg_e[rows, :] = jnp.where(x_even, right, left)
            msg_o[rows, :] = jnp.where(x_even, left, right)
            msg_lo[rows, :] = jnp.where(low, right, left)
            msg_hi[rows, :] = jnp.where(low, left, right)


def ghosts(side, out0, out1, og_ext, stat, nxt):
    lane = lanes()
    column = lane % 4
    span = SIDE_ROWS

    def rows_of(slot, plane, row):
        return side[pl.ds(PAD + slot * span + plane * EXT + row, 8), :]

    for g in range(3):
        row = 8 * g
        away = stat[pl.ds(2 * EXT + row, 8), :]
        for plane in range(PLANES):
            at = pl.ds(plane * EXT + row, 8)
            value = og_ext[at, :]
            out1[at, :] = value
            for d in range(1, REACH + 1):
                source = jnp.where(column == 1, rows_of(REACH - d, plane, row), rows_of(REACH + d, plane, row))
                value = jnp.where(away == d, source, value)
            out0[at, :] = value
        for d in range(1, REACH + 1):
            stat_l = rows_of(REACH - d, PLANES, row)
            stat_r = rows_of(REACH + d, PLANES, row)
            from_left = column < 2

            def both(i):
                return jnp.where(
                    from_left,
                    jnp.broadcast_to(stat_l[:, i : i + 1], (8, COLS)),
                    jnp.broadcast_to(stat_r[:, i : i + 1], (8, COLS)),
                )

            wet, mix = both(0), both(1)
            east_off = jnp.broadcast_to(stat_l[:, 2:3], (8, COLS))
            west_off = jnp.broadcast_to(stat_r[:, 2:3], (8, COLS))
            kmix = wet * mix
            centre = wet - 4.0 * TIME_STEP * wet - 2.0 * kmix
            base = TIME_STEP * wet

            def joined(plane, row):
                return jnp.where(from_left, rows_of(REACH - d, plane, row), rows_of(REACH + d, plane, row))

            here = [joined(plane, row) for plane in range(PLANES)]
            for h in range(2):
                cu = TURN * wet * here[h * FIELDS + 2]
                cv = TURN * wet * here[h * FIELDS + 3]
                ke, kw, kn, ks = base - cu, base + cu, base - cv, base + cv
                for f in range(FIELDS):
                    plane = h * FIELDS + f
                    q = here[plane]
                    edge_e = rows_of(REACH - d, plane, row)
                    edge_w = rows_of(REACH + d, plane, row)
                    east_ghost = jnp.zeros_like(q)
                    west_ghost = jnp.zeros_like(q)
                    for e in range(1, REACH + 1):
                        east_ghost = jnp.where(east_off == e, rows_of(REACH - d + e, plane, row), east_ghost)
                        west_ghost = jnp.where(west_off == e, rows_of(REACH + d - e, plane, row), west_ghost)
                    east_ghost = jnp.where(
                        east_off == 0, pltpu.roll(edge_e, COLS - 2, 1), pltpu.roll(east_ghost, COLS - 1, 1)
                    )
                    west_ghost = jnp.where(
                        west_off == 0, pltpu.roll(edge_w, 2, 1), pltpu.roll(west_ghost, 1, 1)
                    )
                    east = jnp.where(column == 1, east_ghost, pltpu.roll(q, COLS - 1, 1))
                    west = jnp.where(column == 2, west_ghost, pltpu.roll(q, 1, 1))
                    north, south = joined(plane, row + 1), joined(plane, row - 1)
                    other = here[(1 - h) * FIELDS + f]
                    if h == 0:
                        above = jnp.where(lane < 4, q, pltpu.roll(q, 4, 1))
                        below = pltpu.roll(jnp.where(lane < 4, other, q), COLS - 4, 1)
                    else:
                        above = pltpu.roll(jnp.where(lane >= COLS - 4, other, q), 4, 1)
                        below = jnp.where(lane >= COLS - 4, q, pltpu.roll(q, COLS - 4, 1))
                    new = centre * q + ke * east + kw * west + kn * north + ks * south + kmix * (above + below)
                    if f == 2:
                        new = new + cv
                    if f == 3:
                        new = new - cu
                    at = pl.ds(plane * EXT + row, 8)
                    out1[at, :] = jnp.where(away == d, new, out1[at, :])


def substep(src, dst_store, ghost, stat, starts, pack):
    lane = lanes()
    first_lane, last_lane = lane == 0, lane == COLS - 1
    for row in starts:
        wet = stat[pl.ds(row, 8), :]
        mix = stat[pl.ds(EXT + row, 8), :]
        kmix = wet * mix
        centre = wet - 4.0 * TIME_STEP * wet - 2.0 * kmix
        base = TIME_STEP * wet
        turn = TURN * wet

        def load(f, k, shift=0, row=row):
            return src[pl.ds(PAD + (f * LEVELS + k) * EXT + row + shift, 8), :]

        cur = tuple(load(f, 0) for f in range(FIELDS))
        carry = (cur, cur)
        for h in range(2):
            ghost_h = [ghost[pl.ds((h * FIELDS + f) * EXT + row, 8), :] for f in range(FIELDS)]

            def body(i, state, h=h, ghost_h=ghost_h, row=row):
                prev, cur, acc = state
                acc = list(acc)
                for j in range(UNROLL):
                    kk = i * UNROLL + j
                    k = h * HALF + kk
                    nxt = tuple(load(f, jnp.minimum(k + 1, LEVELS - 1)) for f in range(FIELDS))
                    cu, cv = turn * cur[2], turn * cur[3]
                    ke, kw, kn, ks = base - cu, base + cu, base - cv, base + cv
                    for f in range(FIELDS):
                        q = cur[f]
                        edge = pltpu.roll(ghost_h[f], COLS - 2 - 4 * kk, 1)
                        west = pltpu.roll(jnp.where(last_lane, edge, q), 1, 1)
                        east = pltpu.roll(jnp.where(first_lane, edge, q), COLS - 1, 1)
                        north, south = load(f, k, 1), load(f, k, -1)
                        new = (centre * q + ke * east) + (kw * west + kn * north)
                        new = new + (ks * south + kmix * (prev[f] + nxt[f]))
                        if f == 2:
                            new = new + cv
                        if f == 3:
                            new = new - cu
                        dst_store(f, k, row, new)
                        if pack is not None:
                            acc[f] = pack_into(acc[f], new, kk, lane)
                    prev, cur = cur, nxt
                return prev, cur, tuple(acc)

            zero = tuple(jnp.zeros((8, COLS), jnp.float32) for _ in range(FIELDS if pack is not None else 0))
            prev, cur, acc = lax.fori_loop(0, HALF // UNROLL, body, carry + (zero,))
            carry = (prev, cur)
            if pack is not None:
                for f in range(FIELDS):
                    pack[pl.ds((h * FIELDS + f) * EXT + row, 8), :] = acc[f]


def store_in(ref):
    def store(f, k, row, value):
        ref[pl.ds(PAD + (f * LEVELS + k) * EXT + row, 8), :] = value

    return store


def clear_pads(*refs):
    for ref in refs:
        rows = ref.shape[0]
        ref[pl.ds(0, PAD), :] = jnp.zeros((PAD, COLS), jnp.float32)
        ref[pl.ds(rows - PAD, PAD), :] = jnp.zeros((PAD, COLS), jnp.float32)


def first_kernel(sc, ext, own, og_ext, stat, r0, r1, r2, r3, r4, r5, out, pack, side, mid, gh0, gh1):
    clear_pads(side, mid, out)
    side[pl.ds(PAD + REACH * SIDE_ROWS, PACK_ROWS), :] = own[...]
    side[pl.ds(PAD + REACH * SIDE_ROWS + PACK_ROWS, EXT), :] = jnp.zeros((EXT, COLS), jnp.float32)
    for j, r in enumerate((r0, r1, r2, r3, r4, r5)):
        at = pl.multiple_of(PAD + sc[S_SLOT + j] * SIDE_ROWS, 8)
        side[pl.ds(at, SIDE_ROWS), :] = r[...]
    ghosts(side, gh0, gh1, og_ext, stat, None)
    substep(ext, store_in(mid), gh0, stat, (0, 8, 16), None)
    substep(mid, store_in(out), gh1, stat, (0, 8, 16), pack)


def second_kernel(
    sc, ext, own, og_ext, stat, r0, r1, r2, r3, r4, r5, s0, s1, s2, s3, s4, s5,
    out, means, side, mid, gh0, gh1,
):
    clear_pads(side, mid)
    side[pl.ds(PAD + REACH * SIDE_ROWS, PACK_ROWS), :] = own[...]
    side[pl.ds(PAD + REACH * SIDE_ROWS + PACK_ROWS, EXT), :] = jnp.zeros((EXT, COLS), jnp.float32)
    column = lax.broadcasted_iota(jnp.int32, (EXT, COLS), 1) % 4
    for j, (r, s) in enumerate(zip((r0, r1, r2, r3, r4, r5), (s0, s1, s2, s3, s4, s5))):
        slot = sc[S_SLOT + j]
        at = PAD + slot * SIDE_ROWS
        kept = column == jnp.where(slot > REACH, 0, 3)
        for plane in range(PLANES):
            rows = pl.ds(plane * EXT, EXT)
            side[pl.ds(pl.multiple_of(at + plane * EXT, 8), EXT), :] = jnp.where(kept, r[rows, :], s[rows, :])
        side[pl.ds(pl.multiple_of(at + PACK_ROWS, 8), EXT), :] = r[pl.ds(PACK_ROWS, EXT), :]
    ghosts(side, gh0, gh1, og_ext, stat, None)
    substep(ext, store_in(mid), gh0, stat, (0, 8, 16), None)

    def store_out(f, k, row, value):
        out[pl.ds((f * LEVELS + k) * ROWS + row - HALO, 8), :] = value

    substep(mid, store_out, gh1, stat, (HALO, HALO + 8), None)

    source = lax.broadcasted_iota(jnp.int32, (COLS, COLS), 0)
    target = lax.broadcasted_iota(jnp.int32, (COLS, COLS), 1)
    block = 64
    for b in range(FIELDS * LEVELS // block):
        total = jnp.zeros((block, COLS), jnp.float32)
        for a in range(4):
            rows = []
            for c in range(block // 8):
                at = (b * block + c * 8) * ROWS + 4 * a
                part = [out[pl.ds(at + i, 8, stride=ROWS), :] for i in range(4)]
                rows.append((part[0] + part[1]) + (part[2] + part[3]))
            gather = jnp.where(a * 32 + source // 4 == target, 1.0 / 16.0, 0.0).astype(jnp.float32)
            total = total + lax.dot_general(
                jnp.concatenate(rows, axis=0), gather, (((1,), (0,)), ((), ())),
                precision=lax.Precision.HIGHEST, preferred_element_type=jnp.float32,
            )
        means[pl.ds(b * block, block), :] = total


def call(kernel, outs, scratch, *args):
    return pl.pallas_call(
        kernel,
        out_shape=[jax.ShapeDtypeStruct(s, jnp.float32) for s in outs],
        in_specs=[pl.BlockSpec(memory_space=pltpu.SMEM)] + [pl.BlockSpec(memory_space=pltpu.VMEM)] * (len(args) - 1),
        out_specs=[pl.BlockSpec(memory_space=pltpu.VMEM)] * len(outs),
        scratch_shapes=[pltpu.VMEM(s, jnp.float32) for s in scratch],
        compiler_params=pltpu.CompilerParams(vmem_limit_bytes=VMEM_BYTES),
    )(*args)


def per_device(nest_state, mixing, land_mask, face_off, parent_state, parent_block, interp_idx, interp_w):
    tiles = lax.axis_size("nest")
    blocks = lax.axis_size("parent")
    n = lax.axis_index("nest")
    p = lax.axis_index("parent")
    x = n % GROUP
    own_block = parent_block[0, 0]

    def inside(code):
        return [(s, s ^ code) for s in range(tiles)]

    def across(pairs):
        links = []
        for g in range(tiles // GROUP):
            for a, b in pairs:
                i, j = GROUP * g + a, (GROUP * (g + 1) + b) % tiles
                links += [(i, j), (j, i)]
        return links

    rows_1 = [(s, s ^ 1) for s in range(blocks)]
    rows_2 = [(s, ((s + 1) ^ 1) - 1) if 0 < s < blocks - 1 else (s, blocks - 1 - s) for s in range(blocks)]
    links = [
        inside(1), inside(2), inside(3),
        across([(3, 0), (2, 1)]), across([(3, 1), (2, 0)]), across([(3, 2), (1, 0)]),
    ]
    x_even, low = x % 2 == 0, x < 2
    rel = [
        jnp.where(x_even, 1, -1),
        jnp.where(low, 2, -2),
        3 - 2 * x,
        jnp.where(low, -1 - 2 * x, 7 - 2 * x),
        jnp.where(low, -2, 2),
        jnp.where(x_even, -3, 3),
    ]
    sc = jnp.stack(
        [
            (p % 2 == 0).astype(jnp.int32),
            (p > 0).astype(jnp.int32),
            (p < blocks - 1).astype(jnp.int32),
            own_block ^ n,
        ]
        + [REACH + r for r in rel]
        + [x_even.astype(jnp.int32), low.astype(jnp.int32), own_block]
    ).astype(jnp.int32)

    nest2 = nest_state.reshape(FIELDS * LEVELS * ROWS, COLS)
    coarse = parent_state.reshape(FIELDS * LEVELS, COLS)
    halo_rows = (FIELDS * LEVELS * HALO, COLS)
    pay1, pay2 = call(send_rows_kernel, [halo_rows] * 2, [], sc, nest2)
    wide1 = lax.ppermute(pay1, "parent", rows_1)
    wide2 = lax.ppermute(pay2, "parent", rows_2)
    got = [lax.ppermute(coarse, "nest", links[i]) for i in range(3)]
    edge_rows = ((PLANES + 3) * HALO, COLS)
    og, off, epay1, epay2 = call(
        open_kernel, [(PLANES * ROWS, COLS), (ROWS, COLS), edge_rows, edge_rows], [],
        sc, coarse, *got, interp_idx.reshape(ROWS, 8), interp_w.reshape(ROWS, 8), face_off, land_mask, mixing,
    )
    edge1 = lax.ppermute(epay1, "parent", rows_1)
    edge2 = lax.ppermute(epay2, "parent", rows_2)
    side = (SIDE_ROWS, COLS)
    ext, pack, og_ext, stat, msg_e, msg_o, msg_lo, msg_hi = call(
        extend_kernel,
        [(STATE_ROWS, COLS), (PACK_ROWS, COLS), (PACK_ROWS, COLS), (3 * EXT, COLS)] + [side] * 4, [],
        sc, nest2, wide1, wide2, og, off, land_mask, mixing, edge1, edge2,
    )
    msgs = [msg_e, msg_lo, msg_lo, msg_hi, msg_hi, msg_o]
    first = [lax.ppermute(m, "nest", link) for m, link in zip(msgs, links)]
    work = [(SLOTS * SIDE_ROWS + 2 * PAD, COLS), (STATE_ROWS, COLS), (PACK_ROWS, COLS), (PACK_ROWS, COLS)]
    ext, pack = call(
        first_kernel, [(STATE_ROWS, COLS), (PACK_ROWS, COLS)], work, sc, ext, pack, og_ext, stat, *first
    )
    second = [lax.ppermute(pack, "nest", link) for link in links]
    new2, means = call(
        second_kernel, [(FIELDS * LEVELS * ROWS, COLS), (FIELDS * LEVELS, COLS)], work,
        sc, ext, pack, og_ext, stat, *first, *second,
    )
    received = means
    me = n.astype(jnp.float32)
    for i in range(3):
        arrived = lax.ppermute(means, "nest", links[i])
        received = jnp.where(first[i][PACK_ROWS, 3] == me, arrived, received)
    parent_new = coarse + FEEDBACK * (received - coarse)
    return new2.reshape(nest_state.shape), parent_new.reshape(parent_state.shape)


def solution(mesh):
    return jax.shard_map(
        per_device,
        mesh=mesh,
        in_specs=(
            P(None, None, "parent", "nest"),
            P("parent", "nest"),
            P("parent", "nest"),
            P("parent", "nest"),
            P(None, None, "parent", "nest"),
            P("parent", "nest"),
            P("parent", "nest", None),
            P("parent", "nest", None),
        ),
        out_specs=(P(None, None, "parent", "nest"), P(None, None, "parent", "nest")),
        check_vma=False,
    )
```

```python
import jax
import jax.numpy as jnp
from jax import lax
from jax.experimental import pallas as pl
from jax.experimental.pallas import tpu as pltpu
from jax.sharding import PartitionSpec as P

FIELDS = 4
LEVELS = 64
ROWS = 16
COLS = 128
HALO = 4
EXT = ROWS + 2 * HALO
YB = 3
YC = 8
KB = 4
KA = 16
BLOCKS = YB * FIELDS * KB
PAD = 8
STATE_ROWS = BLOCKS * COLS + 2 * PAD
SIDE_ROWS = 4 * BLOCKS + 16
WIDE_ROWS = FIELDS * LEVELS * HALO
REACH = 3
SLOTS = 2 * REACH + 1
GROUP = 4
VMEM_BYTES = 44 * 1024 * 1024

TIME_STEP = 0.1
TURN = 0.05
FEEDBACK = 0.5
HIGHEST = lax.Precision.HIGHEST

S_EVEN, S_TOP, S_BOTTOM, S_PBX, S_SLOT, S_XEVEN, S_LOW, S_PB, S_ME = 0, 1, 2, 3, 4, 10, 11, 12, 13


def lanes(rows=8):
    return lax.broadcasted_iota(jnp.int32, (rows, COLS), 1)


def sublanes(rows=8):
    return lax.broadcasted_iota(jnp.int32, (rows, COLS), 0)


def wide(row):
    return jnp.broadcast_to(row, (8, COLS))


def unrolled(count, step, body):
    def several(i, carry):
        for j in range(step):
            body(i * step + j)
        return carry

    lax.fori_loop(0, count // step, several, 0)


def rows_kernel(sc, far_nest, mask, mixing, pay1, pay2, nest, wet, mix, sems):
    share = LEVELS * ROWS
    copies = [
        pltpu.make_async_copy(far_nest.at[pl.ds(f * share, share)], nest.at[pl.ds(f * share, share)], sems.at[f])
        for f in range(FIELDS)
    ]
    copies += [
        pltpu.make_async_copy(mask, wet, sems.at[FIELDS]),
        pltpu.make_async_copy(mixing, mix, sems.at[FIELDS + 1]),
    ]
    for copy in copies:
        copy.start()
    even = sc[S_EVEN] == 1
    first = jnp.where(even, ROWS - HALO, 0)
    second = jnp.where(even, 0, ROWS - HALO)
    for f in range(FIELDS):
        copies[f].wait()

        def move(i, f=f):
            at, to = (f * LEVELS + i) * ROWS, (f * LEVELS + i) * HALO
            pay1[pl.ds(to, HALO), :] = nest[pl.ds(at + first, HALO), :]
            pay2[pl.ds(to, HALO), :] = nest[pl.ds(at + second, HALO), :]

        unrolled(LEVELS, 16, move)
    copies[FIELDS].wait()
    copies[FIELDS + 1].wait()
    for i, plane in enumerate((wet[...].astype(jnp.float32), mix[...])):
        low, high = plane[:HALO], plane[ROWS - HALO :]
        pay1[pl.ds(WIDE_ROWS + i * HALO, HALO), :] = jnp.where(even, high, low)
        pay2[pl.ds(WIDE_ROWS + i * HALO, HALO), :] = jnp.where(even, low, high)


def table_kernel(coarse, face, idx, weight, table, offs, kept, spread, near, face_in, idx_in, weight_in, sems):
    pairs = ((coarse, near), (face, face_in), (idx, idx_in), (weight, weight_in))
    copies = [pltpu.make_async_copy(far, here, sems.at[i]) for i, (far, here) in enumerate(pairs)]
    for copy in copies:
        copy.start()
    for copy in copies:
        copy.wait()
    kept[...] = near[...]

    def upright(small):
        spread[pl.ds(0, 8), :] = jnp.zeros((8, COLS), jnp.float32)
        spread[pl.ds(0, small.shape[0]), 0:ROWS] = small.astype(jnp.float32)
        return spread[pl.ds(0, 8), :].T[:ROWS]

    face = upright(face_in[...])
    idx = upright(idx_in[...])
    weight = upright(weight_in[...])
    offs[pl.ds(0, ROWS), :] = jnp.broadcast_to(face[:, 0:1], (ROWS, COLS))
    offs[pl.ds(ROWS, ROWS), :] = jnp.broadcast_to(face[:, 1:2], (ROWS, COLS))
    cell = lanes(ROWS).astype(jnp.float32)
    spread[...] = jnp.zeros_like(spread)
    for side in range(2):
        total = jnp.zeros((ROWS, 1), jnp.float32)
        values = jnp.zeros((ROWS, COLS), jnp.float32)
        for j in range(4):
            c = side * 4 + j
            w = weight[:, c : c + 1]
            total = total + w
            values = values + jnp.where(idx[:, c : c + 1] == cell, w, 0.0)
        spread[pl.ds(side * EXT + HALO, ROWS), :] = values / total
    for side in range(2):
        for yb in range(YB):
            table[pl.ds(side * EXT + yb * YC, YC), :] = spread[pl.ds(side * EXT + yb, YC, stride=YB), :]


def open_kernel(sc, own, got1, got2, got3, table, offs, og, chosen):
    og[pl.ds(2 * BLOCKS, 2 * ROWS), :] = offs[...]
    pbx = sc[S_PBX]
    value = own[...]
    for code, got in ((1, got1), (2, got2), (3, got3)):
        value = jnp.where(pbx == code, got[...], value)
    chosen[...] = value
    rows = []
    for f in range(FIELDS):
        for kb in range(KB):
            for a in range(2):
                rows.append(chosen[pl.ds(f * LEVELS + kb + a * 8 * KB, 8, stride=KB), :])
    weights = jnp.concatenate([table[...], jnp.zeros((COLS - 2 * EXT, COLS), jnp.float32)], axis=0)
    values = lax.dot_general(
        jnp.concatenate(rows, axis=0), weights, (((1,), (1,)), ((), ())),
        precision=HIGHEST, preferred_element_type=jnp.float32,
    )
    shift = (lanes() // KA - sublanes()) % 8
    for half in range(2):
        upright = values[half * COLS : (half + 1) * COLS].T
        for i in range(2 * YB):
            part = upright[i * YC : (i + 1) * YC]
            value = part
            for d in range(1, 8):
                value = jnp.where(shift == d, pltpu.roll(pltpu.roll(part, KA * d, 1), 8 - d, 0), value)
            og[pl.ds(i * 16 + half * 8, 8), :] = value


def columns_of(state, edges):
    for c, x in enumerate((COLS - 1, 0, COLS - 2, 1)):
        for i in range(BLOCKS // 8):
            edges[pl.ds(c * BLOCKS + 8 * i, 8), :] = state[pl.ds(PAD + 8 * i * COLS + x, 8, stride=COLS), :]


def halos(sc, one, two):
    even = sc[S_EVEN] == 1
    top = jnp.where(sc[S_TOP] == 1, jnp.where(even, two, one), 0.0)
    bottom = jnp.where(sc[S_BOTTOM] == 1, jnp.where(even, one, two), 0.0)
    return top, bottom


def turn_kernel(sc, nest, wide1, wide2, far_mask, far_mixing, state, coef, edges, ext, mask, mixing, sems):
    copies = [
        pltpu.make_async_copy(far_mask, mask, sems.at[0]),
        pltpu.make_async_copy(far_mixing, mixing, sems.at[1]),
    ]
    for copy in copies:
        copy.start()
    pad = jnp.zeros((PAD, COLS), jnp.float32)
    state[pl.ds(0, PAD), :] = pad
    state[pl.ds(STATE_ROWS - PAD, PAD), :] = pad
    even = sc[S_EVEN] == 1
    top_in, bottom_in = sc[S_TOP] == 1, sc[S_BOTTOM] == 1
    for yb in range(YB):

        def tile(i, yb=yb):
            base = (i // KB) * LEVELS + i % KB
            rows = []
            for yc in range(YC):
                r = YB * yc + yb
                for a in range(2):
                    level = base + a * 8 * KB
                    if HALO <= r < HALO + ROWS:
                        rows.append(nest[pl.ds(level * ROWS + r - HALO, 8, stride=KB * ROWS), :])
                    else:
                        at = pl.ds(level * HALO + r % ROWS % HALO, 8, stride=KB * HALO)
                        one, two = wide1[at, :], wide2[at, :]
                        if r < HALO:
                            rows.append(jnp.where(top_in, jnp.where(even, two, one), 0.0))
                        else:
                            rows.append(jnp.where(bottom_in, jnp.where(even, one, two), 0.0))
            at = pl.multiple_of(PAD + (yb * 16 + i) * COLS, 8)
            state[pl.ds(at, COLS), :] = jnp.concatenate(rows, axis=0).T

        unrolled(16, TILES, tile)
    for copy in copies:
        copy.wait()
    for i, plane in enumerate((mask[...].astype(jnp.float32), mixing[...])):
        at = pl.ds(WIDE_ROWS + i * HALO, HALO)
        top, bottom = halos(sc, wide1[at, :], wide2[at, :])
        ext[pl.ds(i * EXT, HALO), :] = top
        ext[pl.ds(i * EXT + HALO, ROWS), :] = plane
        ext[pl.ds(i * EXT + HALO + ROWS, HALO), :] = bottom
    for yb in range(YB):
        for i in range(2):
            rows = [
                jnp.broadcast_to(ext[pl.ds(i * EXT + YB * yc + yb, 1), :], (KA, COLS)) for yc in range(YC)
            ]
            coef[pl.ds((i * YB + yb) * COLS, COLS), :] = jnp.concatenate(rows, axis=0).T
    columns_of(state, edges)


def message_kernel(sc, edges, og, edge1, edge2, coef, ogx, offv, msg_e, msg_o, msg_lo, msg_hi, left, right, ext):
    mine = sublanes() == lanes() // KA
    even = sc[S_EVEN] == 1
    for i in range(2):
        at = 2 * BLOCKS + i * ROWS
        one_low, one_high = edge1[pl.ds(at, HALO), :], edge1[pl.ds(at + ROWS - HALO, HALO), :]
        two_low, two_high = edge2[pl.ds(at, HALO), :], edge2[pl.ds(at + ROWS - HALO, HALO), :]
        ext[pl.ds(i * EXT, HALO), :] = jnp.where(even, two_high, one_high)
        ext[pl.ds(i * EXT + HALO, ROWS), :] = og[pl.ds(at, ROWS), :]
        ext[pl.ds(i * EXT + HALO + ROWS, HALO), :] = jnp.where(even, one_low, two_low)
        for yb in range(YB):
            away = ext[pl.ds(i * EXT + yb, YC, stride=YB), :]
            offv[pl.ds(i * YB + yb, 1), :] = jnp.sum(jnp.where(mine, away, 0.0), axis=0, keepdims=True)
    lane16 = lanes(16) // KA
    for side in range(2):
        tops, bottoms = [], []
        for yb in range(YB):
            rows = pl.ds((side * YB + yb) * 16, 16)
            top, bottom = halos(sc, edge1[rows, :], edge2[rows, :])
            tops.append(top)
            bottoms.append(bottom)
        for yb in range(YB):
            rows = pl.ds((side * YB + yb) * 16, 16)
            row = YB * lane16 + yb
            up = pltpu.roll(tops[(yb + 1) % YB], COLS - KA * (6 if yb == 2 else 5), 1)
            down = pltpu.roll(bottoms[(yb + 2) % YB], KA * (6 if yb == 0 else 5), 1)
            ogx[rows, :] = jnp.where(row < HALO, up, jnp.where(row >= HALO + ROWS, down, og[rows, :]))
    number = sc[S_PB].astype(jnp.float32)
    for ref, third, opened, x, off in ((right, 2, 1, COLS - 1, 1), (left, 3, 0, 0, 0)):
        ref[pl.ds(0, 2 * BLOCKS), :] = edges[pl.ds(0, 2 * BLOCKS), :]
        ref[pl.ds(2 * BLOCKS, BLOCKS), :] = edges[pl.ds(third * BLOCKS, BLOCKS), :]
        ref[pl.ds(3 * BLOCKS, BLOCKS), :] = ogx[pl.ds(opened * BLOCKS, BLOCKS), :]
        ref[pl.ds(4 * BLOCKS, 16), :] = jnp.zeros((16, COLS), jnp.float32) + number
        for i in range(2 * YB):
            ref[pl.ds(4 * BLOCKS + i, 1), :] = coef[pl.ds(i * COLS + x, 1), :]
        ref[pl.ds(4 * BLOCKS + 2 * YB, YB), :] = offv[pl.ds(off * YB, YB), :]
    x_even, low = sc[S_XEVEN] == 1, sc[S_LOW] == 1
    msg_e[...] = jnp.where(x_even, right[...], left[...])
    msg_o[...] = jnp.where(x_even, left[...], right[...])
    msg_lo[...] = jnp.where(low, right[...], left[...])
    msg_hi[...] = jnp.where(low, left[...], right[...])


def coefficients(wet, mix):
    kmix = wet * mix
    return kmix, wet - 4.0 * TIME_STEP * wet - 2.0 * kmix, TIME_STEP * wet, TURN * wet


def advance_edge(q, east, west, wet, mix):
    sub, lane = sublanes(), lanes() % KA
    new = []
    for yb in range(YB):
        kmix, centre, base, turn = coefficients(wide(wet[yb]), wide(mix[yb]))
        flow = q[yb][1]
        swapped = pltpu.roll(flow, 4, 0)
        cu = turn * jnp.where(sub < 4, flow, swapped)
        cv = turn * jnp.where(sub < 4, swapped, flow)
        pair = []
        for half in range(2):
            c = q[yb][half]
            above = jnp.where(
                sub % KB >= 1, pltpu.roll(c, 1, 0),
                jnp.where(lane == 0, c, pltpu.roll(pltpu.roll(c, 5, 0), 1, 1)),
            )
            below = jnp.where(
                sub % KB < KB - 1, pltpu.roll(c, 7, 0),
                jnp.where(lane == KA - 1, c, pltpu.roll(pltpu.roll(c, 3, 0), COLS - 1, 1)),
            )
            south = q[yb - 1][half] if yb > 0 else pltpu.roll(q[YB - 1][half], KA, 1)
            north = q[yb + 1][half] if yb < YB - 1 else pltpu.roll(q[0][half], COLS - KA, 1)
            value = (centre * c + (base - cu) * east[yb][half]) + ((base + cu) * west[yb][half] + (base - cv) * north)
            value = value + ((base + cv) * south + kmix * (above + below))
            if half == 1:
                value = value + jnp.where(sub < 4, cv, -cu)
            pair.append(value)
        new.append(pair)
    return new


def ghosts(side, ogx, offv, west0, east0, west1, east1):
    def column(slot, c):
        return [
            [side[pl.ds(slot * SIDE_ROWS + c * BLOCKS + yb * 16 + half * 8, 8), :] for half in range(2)]
            for yb in range(YB)
        ]

    def fact(slot, i):
        return [side[pl.ds(slot * SIDE_ROWS + 4 * BLOCKS + i * YB + yb, 1), :] for yb in range(YB)]

    def pick(away, choices, value):
        for e, choice in choices:
            value = [
                [jnp.where(wide(away[yb]) == e, choice[yb][half], value[yb][half]) for half in range(2)]
                for yb in range(YB)
            ]
        return value

    def put(ref, value):
        for yb in range(YB):
            for half in range(2):
                ref[pl.ds(yb * 16 + half * 8, 8), :] = value[yb][half]

    for sign, first, second in ((-1, west0, west1), (1, east0, east1)):
        which = 0 if sign < 0 else 1
        away = [offv[pl.ds(which * YB + yb, 1), :] for yb in range(YB)]
        opened = [
            [ogx[pl.ds(which * BLOCKS + yb * 16 + half * 8, 8), :] for half in range(2)] for yb in range(YB)
        ]
        reach = range(1, REACH + 1)
        put(first, pick(away, [(d, column(REACH + sign * d, which)) for d in reach], opened))
        later = opened
        for d in reach:
            slot = REACH + sign * d
            outer = pick(
                fact(slot, 2), [(e, column(slot - sign * e, 1 - which)) for e in reach], column(slot, 3)
            )
            inner = column(slot, 2)
            east, west = (outer, inner) if sign < 0 else (inner, outer)
            new = advance_edge(column(slot, which), east, west, fact(slot, 0), fact(slot, 1))
            later = pick(away, [(d, new)], later)
        put(second, later)


def substep(src, dst, west_ghost, east_ghost, coef):
    sub, ka = sublanes(), lanes() % KA

    def block(yb, f, kb):
        return (yb * FIELDS + f) * KB + kb

    for yb in range(YB):

        def group(xg, first, last, yb=yb):
            x = xg * 8

            def load(yb, f, kb, shift=0):
                return src[pl.ds(PAD + block(yb, f, kb) * COLS + x + shift, 8), :]

            kmix, centre, base, turn = coefficients(
                coef[pl.ds(yb * COLS + x, 8), :], coef[pl.ds((YB + yb) * COLS + x, 8), :]
            )
            q = [[load(yb, f, kb) for kb in range(KB)] for f in range(FIELDS)]
            for kb in range(KB):
                cu, cv = turn * q[2][kb], turn * q[3][kb]
                ke, kw, kn, ks = base - cu, base + cu, base - cv, base + cv
                for f in range(FIELDS):
                    c = q[f][kb]
                    b = block(yb, f, kb)
                    west, east = load(yb, f, kb, -1), load(yb, f, kb, 1)
                    if first:
                        west = jnp.where(sub == 0, wide(west_ghost[pl.ds(b, 1), :]), west)
                    if last:
                        east = jnp.where(sub == 7, wide(east_ghost[pl.ds(b, 1), :]), east)
                    south = load(yb - 1, f, kb) if yb > 0 else pltpu.roll(load(YB - 1, f, kb), KA, 1)
                    north = load(yb + 1, f, kb) if yb < YB - 1 else pltpu.roll(load(0, f, kb), COLS - KA, 1)
                    above = q[f][kb - 1] if kb > 0 else jnp.where(ka == 0, c, pltpu.roll(q[f][KB - 1], 1, 1))
                    below = q[f][kb + 1] if kb < KB - 1 else jnp.where(ka == KA - 1, c, pltpu.roll(q[f][0], COLS - 1, 1))
                    new = (centre * c + ke * east) + (kw * west + kn * north)
                    new = new + (ks * south + kmix * (above + below))
                    if f == 2:
                        new = new + cv
                    if f == 3:
                        new = new - cu
                    dst[pl.ds(PAD + b * COLS + x, 8), :] = new

        group(0, True, False)

        def body(i, carry, group=group):
            for j in range(UNROLL):
                group(1 + i * UNROLL + j, False, False)
            return carry

        lax.fori_loop(0, (COLS // 8 - 2) // UNROLL, body, 0)
        group(COLS // 8 - 1, False, True)


UNROLL = 2
TILES = 4


def clear_pads(*refs):
    for ref in refs:
        ref[pl.ds(0, PAD), :] = jnp.zeros((PAD, COLS), jnp.float32)
        ref[pl.ds(STATE_ROWS - PAD, PAD), :] = jnp.zeros((PAD, COLS), jnp.float32)


def first_kernel(
    sc, state, own, ogx, coef, offv, r0, r1, r2, r3, r4, r5, out, edges, side, mid, west0, east0, west1, east1
):
    clear_pads(mid, out)
    side[pl.ds(REACH * SIDE_ROWS, 2 * BLOCKS), :] = own[pl.ds(0, 2 * BLOCKS), :]
    for j, r in enumerate((r0, r1, r2, r3, r4, r5)):
        side[pl.ds(pl.multiple_of(sc[S_SLOT + j] * SIDE_ROWS, 8), SIDE_ROWS), :] = r[...]
    ghosts(side, ogx, offv, west0, east0, west1, east1)
    substep(state, mid, west0, east0, coef)
    substep(mid, out, west1, east1, coef)
    columns_of(out, edges)


def second_kernel(
    sc, state, own, ogx, coef, offv, r0, r1, r2, r3, r4, r5, s0, s1, s2, s3, s4, s5,
    out, means, blocks, side, mid, west0, east0, west1, east1, end, nat, sems,
):
    clear_pads(mid)
    side[pl.ds(REACH * SIDE_ROWS, 2 * BLOCKS), :] = own[pl.ds(0, 2 * BLOCKS), :]
    for j, (r, s) in enumerate(zip((r0, r1, r2, r3, r4, r5), (s0, s1, s2, s3, s4, s5))):
        slot = sc[S_SLOT + j]
        at = slot * SIDE_ROWS
        third = pl.multiple_of(jnp.where(slot > REACH, 3 * BLOCKS, 2 * BLOCKS), 8)
        side[pl.ds(pl.multiple_of(at, 8), 2 * BLOCKS), :] = s[pl.ds(0, 2 * BLOCKS), :]
        side[pl.ds(pl.multiple_of(at + 2 * BLOCKS, 8), BLOCKS), :] = s[pl.ds(third, BLOCKS), :]
        side[pl.ds(pl.multiple_of(at + 3 * BLOCKS, 8), BLOCKS + 16), :] = r[pl.ds(3 * BLOCKS, BLOCKS + 16), :]
    ghosts(side, ogx, offv, west0, east0, west1, east1)
    substep(state, mid, west0, east0, coef)
    substep(mid, end, west1, east1, coef)
    for j in range(3):
        blocks[pl.ds(j * 8, 8), :] = wide((r0, r1, r2)[j][pl.ds(SIDE_ROWS - 1, 1), :])
    share = LEVELS * ROWS
    copies = [
        pltpu.make_async_copy(nat.at[pl.ds(f * share, share)], out.at[pl.ds(f * share, share)], sems.at[f])
        for f in range(FIELDS)
    ]
    for f in range(FIELDS):
        for yb in range(YB):

            def tile(kb, yb=yb, f=f):
                base = f * LEVELS + kb
                block = (yb * FIELDS + f) * KB + kb
                rows = end[pl.ds(pl.multiple_of(PAD + block * COLS, 8), COLS), :].T
                for yc in range(YC):
                    r = YB * yc + yb - HALO
                    if 0 <= r < ROWS:
                        for a in range(2):
                            at = pl.ds((base + a * 8 * KB) * ROWS + r, 8, stride=KB * ROWS)
                            nat[at, :] = rows[yc * KA + 8 * a : yc * KA + 8 * a + 8]

            unrolled(KB, TILES, tile)
        copies[f].start()

    target = lanes(COLS)
    block = 64
    for b in range(FIELDS * LEVELS // block):
        total = jnp.zeros((block, COLS), jnp.float32)
        for a in range(4):
            rows = []
            for c in range(block // 8):
                at = (b * block + c * 8) * ROWS + 4 * a
                part = [nat[pl.ds(at + i, 8, stride=ROWS), :] for i in range(4)]
                rows.append((part[0] + part[1]) + (part[2] + part[3]))
            gather = jnp.where(a * 32 + sublanes(COLS) // 4 == target, 1.0 / 16.0, 0.0).astype(jnp.float32)
            total = total + lax.dot_general(
                jnp.concatenate(rows, axis=0), gather, (((1,), (0,)), ((), ())),
                precision=HIGHEST, preferred_element_type=jnp.float32,
            )
        means[pl.ds(b * block, block), :] = total
    for copy in copies:
        copy.wait()


def feedback_kernel(sc, coarse, means, got1, got2, got3, blocks, out):
    me = sc[S_ME].astype(jnp.float32)
    for i in range(FIELDS * LEVELS // 8):
        rows = pl.ds(i * 8, 8)
        value = means[rows, :]
        for j, got in enumerate((got1, got2, got3)):
            value = jnp.where(blocks[pl.ds(j * 8, 8), :] == me, got[rows, :], value)
        old = coarse[rows, :]
        out[rows, :] = old + FEEDBACK * (value - old)


def call(kernel, outs, scratch, *args, far=(), far_out=()):
    def spec(i, places, arg=None):
        if i in places:
            return pl.BlockSpec(memory_space=pltpu.HBM)
        small = arg is not None and arg.ndim == 1
        return pl.BlockSpec(memory_space=pltpu.SMEM if small else pltpu.VMEM)

    return pl.pallas_call(
        kernel,
        out_shape=[jax.ShapeDtypeStruct(s, jnp.float32) for s in outs],
        in_specs=[spec(i, far, a) for i, a in enumerate(args)],
        out_specs=[spec(i, far_out) for i in range(len(outs))],
        scratch_shapes=[pltpu.VMEM(s, jnp.float32) if isinstance(s, tuple) else s for s in scratch],
        compiler_params=pltpu.CompilerParams(vmem_limit_bytes=VMEM_BYTES),
    )(*args)


def per_device(nest_state, mixing, land_mask, face_off, parent_state, parent_block, interp_idx, interp_w):
    tiles = lax.axis_size("nest")
    blocks = lax.axis_size("parent")
    n = lax.axis_index("nest")
    p = lax.axis_index("parent")
    x = n % GROUP
    own_block = parent_block[0, 0]

    def inside(code):
        return [(s, s ^ code) for s in range(tiles)]

    def across(pairs):
        links = []
        for g in range(tiles // GROUP):
            for a, b in pairs:
                i, j = GROUP * g + a, (GROUP * (g + 1) + b) % tiles
                links += [(i, j), (j, i)]
        return links

    rows_1 = [(s, s ^ 1) for s in range(blocks)]
    rows_2 = [(s, ((s + 1) ^ 1) - 1) if 0 < s < blocks - 1 else (s, blocks - 1 - s) for s in range(blocks)]
    links = [
        inside(1), inside(2), inside(3),
        across([(3, 0), (2, 1)]), across([(3, 1), (2, 0)]), across([(3, 2), (1, 0)]),
    ]
    x_even, low = x % 2 == 0, x < 2
    rel = [
        jnp.where(x_even, 1, -1),
        jnp.where(low, 2, -2),
        3 - 2 * x,
        jnp.where(low, -1 - 2 * x, 7 - 2 * x),
        jnp.where(low, -2, 2),
        jnp.where(x_even, -3, 3),
    ]
    sc = jnp.stack(
        [
            (p % 2 == 0).astype(jnp.int32),
            (p > 0).astype(jnp.int32),
            (p < blocks - 1).astype(jnp.int32),
            own_block ^ n,
        ]
        + [REACH + r for r in rel]
        + [x_even.astype(jnp.int32), low.astype(jnp.int32), own_block, n]
    ).astype(jnp.int32)

    nest2 = nest_state.reshape(FIELDS * LEVELS * ROWS, COLS)
    coarse = parent_state.reshape(FIELDS * LEVELS, COLS)
    natural = (FIELDS * LEVELS * ROWS, COLS)
    rows, narrow = (WIDE_ROWS + 2 * HALO, COLS), (ROWS, COLS)
    pay1, pay2 = call(
        rows_kernel, [rows, rows],
        [natural, pltpu.VMEM(narrow, jnp.int32), pltpu.VMEM(narrow, jnp.float32), pltpu.SemaphoreType.DMA((6,))],
        sc, nest2, land_mask, mixing, far=(1, 2, 3),
    )
    wide1 = lax.ppermute(pay1, "parent", rows_1)
    wide2 = lax.ppermute(pay2, "parent", rows_2[1:-1])
    got = [lax.ppermute(coarse, "nest", links[i]) for i in range(3)]
    face, idx, weight, pay1 = lax.optimization_barrier(
        (face_off.T, interp_idx.transpose(1, 2, 0).reshape(8, ROWS), interp_w.transpose(1, 2, 0).reshape(8, ROWS), pay1)
    )
    coarse_rows = (FIELDS * LEVELS, COLS)
    table, offs, kept = call(
        table_kernel, [(2 * EXT, COLS), (2 * ROWS, COLS), coarse_rows],
        [(2 * EXT, COLS), coarse_rows, pltpu.VMEM((2, ROWS), jnp.int32), pltpu.VMEM((8, ROWS), jnp.int32),
         pltpu.VMEM((8, ROWS), jnp.float32), pltpu.SemaphoreType.DMA((4,))],
        coarse, face, idx, weight, far=(0, 1, 2, 3),
    )
    block, state_rows = (BLOCKS, COLS), (STATE_ROWS, COLS)
    (og,) = call(
        open_kernel, [(2 * BLOCKS + 2 * ROWS, COLS)], [coarse_rows], sc, kept, *got, table, offs
    )
    edge1 = lax.ppermute(og, "parent", rows_1)
    edge2 = lax.ppermute(og, "parent", rows_2)
    state, coef, edges = call(
        turn_kernel, [state_rows, (2 * YB * COLS, COLS), (4 * BLOCKS, COLS)],
        [(2 * EXT, COLS), pltpu.VMEM(narrow, jnp.int32), pltpu.VMEM(narrow, jnp.float32), pltpu.SemaphoreType.DMA((2,))],
        sc, nest2, wide1, wide2, land_mask, mixing, far=(4, 5),
    )
    side = (SIDE_ROWS, COLS)
    ogx, offv, msg_e, msg_o, msg_lo, msg_hi = call(
        message_kernel, [(2 * BLOCKS, COLS), (8, COLS)] + [side] * 4, [side, side, (2 * EXT, COLS)],
        sc, edges, og, edge1, edge2, coef,
    )
    msgs = [msg_e, msg_lo, msg_lo, msg_hi, msg_hi, msg_o]
    first = [lax.ppermute(m, "nest", link) for m, link in zip(msgs, links)]
    work = [(SLOTS * SIDE_ROWS, COLS), state_rows] + [block] * 4
    state, edges = call(
        first_kernel, [state_rows, (4 * BLOCKS, COLS)], work, sc, state, edges, ogx, coef, offv, *first
    )
    second = [lax.ppermute(edges, "nest", link) for link in links]
    new2, means, blocks = call(
        second_kernel, [natural, coarse_rows, (24, COLS)],
        work + [state_rows, natural, pltpu.SemaphoreType.DMA((FIELDS,))],
        sc, state, edges, ogx, coef, offv, *first, *second, far_out=(0,),
    )
    arrived = [lax.ppermute(means, "nest", links[i]) for i in range(3)]
    (parent_new,) = call(feedback_kernel, [coarse_rows], [], sc, kept, means, *arrived, blocks)
    return new2.reshape(nest_state.shape), parent_new.reshape(parent_state.shape)


def solution(mesh):
    return jax.shard_map(
        per_device,
        mesh=mesh,
        in_specs=(
            P(None, None, "parent", "nest"),
            P("parent", "nest"),
            P("parent", "nest"),
            P("parent", "nest"),
            P(None, None, "parent", "nest"),
            P("parent", "nest"),
            P("parent", "nest", None),
            P("parent", "nest", None),
        ),
        out_specs=(P(None, None, "parent", "nest"), P(None, None, "parent", "nest")),
        check_vma=False,
    )
```

```python
import jax
import jax.numpy as jnp
from jax import lax
from jax.experimental import pallas as pl
from jax.experimental.pallas import tpu as pltpu
from jax.sharding import PartitionSpec as P

FIELDS = 4
LEVELS = 64
ROWS = 16
COLS = 128
HALO = 4
EXT = ROWS + 2 * HALO
YB = 3
YC = 8
KB = 4
KA = 16
BLOCKS = YB * FIELDS * KB
PAD = 8
STATE_ROWS = BLOCKS * COLS + 2 * PAD
SIDE_ROWS = 4 * BLOCKS + 16
SHARE = 6 * 16 + 8
SWAP_ROWS = SHARE + 4 * ROWS
WIDE_ROWS = FIELDS * LEVELS * HALO
REACH = 3
SMALL = 1000
SLOTS = 2 * REACH + 1
GROUP = 4
VMEM_BYTES = 44 * 1024 * 1024

TIME_STEP = 0.1
TURN = 0.05
FEEDBACK = 0.5
HIGHEST = lax.Precision.HIGHEST

S_EVEN, S_TOP, S_BOTTOM, S_PBX, S_SLOT, S_XEVEN, S_LOW, S_PB, S_ME = 0, 1, 2, 3, 4, 10, 11, 12, 13


def lanes(rows=8):
    return lax.broadcasted_iota(jnp.int32, (rows, COLS), 1)


def sublanes(rows=8):
    return lax.broadcasted_iota(jnp.int32, (rows, COLS), 0)


def wide(row):
    return jnp.broadcast_to(row, (8, COLS))


def unrolled(count, step, body):
    def several(i, carry):
        for j in range(step):
            body(i * step + j)
        return carry

    lax.fori_loop(0, count // step, several, 0)


def rows_kernel(sc, nest, pay1, pay2):
    even = sc[S_EVEN] == 1
    first = jnp.where(even, ROWS - HALO, 0)
    second = jnp.where(even, 0, ROWS - HALO)

    def move(i):
        at, to = i * ROWS, i * HALO
        pay1[pl.ds(to, HALO), :] = nest[pl.ds(at + first, HALO), :]
        pay2[pl.ds(to, HALO), :] = nest[pl.ds(at + second, HALO), :]

    unrolled(FIELDS * LEVELS, 16, move)


def ends_kernel(nest, mask, mixing, ends, ext):
    nothing = jnp.zeros((8, COLS), jnp.float32)
    ext[...] = jnp.zeros_like(ext)
    planes = (mask[...].astype(jnp.float32), mixing[...])
    for i, plane in enumerate(planes):
        ext[pl.ds(i * EXT + HALO, ROWS), :] = plane
        ends[pl.ds(YB * SHARE + i * ROWS, ROWS), :] = plane
    for yb in range(YB):
        ends[pl.ds(yb * SHARE + 96, 8), :] = nothing
        for i in range(2):
            rows = [jnp.broadcast_to(ext[pl.ds(i * EXT + YB * yc + yb, 1), :], (KA, COLS)) for yc in range(YC)]
            tile = jnp.concatenate(rows, axis=0).T
            ends[pl.ds(yb * SHARE + 96 + i, 1), :] = tile[COLS - 1 : COLS]
            ends[pl.ds(yb * SHARE + 98 + i, 1), :] = tile[0:1]

        def take(i, yb=yb):
            base = (i // KB) * LEVELS + i % KB
            rows = []
            for yc in range(YC):
                r = YB * yc + yb - HALO
                for a in range(2):
                    if 0 <= r < ROWS:
                        rows.append(nest[pl.ds((base + a * 8 * KB) * ROWS + r, 8, stride=KB * ROWS), :])
                    else:
                        rows.append(nothing)
            tile = jnp.concatenate(rows, axis=0).T
            for c, x in enumerate((COLS - 1, 0, COLS - 2, 1)):
                ends[pl.ds(yb * SHARE + c * 16 + i, 1), :] = tile[x : x + 1]

        unrolled(16, TILES, take)


def table_kernel(coarse, face, idx, weight, table, offs, kept, spread, near, face_in, idx_in, weight_in, sems):
    pairs = ((coarse, near), (face, face_in), (idx, idx_in), (weight, weight_in))
    copies = [pltpu.make_async_copy(far, here, sems.at[i]) for i, (far, here) in enumerate(pairs)]
    for copy in copies:
        copy.start()
    for copy in copies:
        copy.wait()
    kept[...] = near[...]

    def upright(small):
        spread[pl.ds(0, 8), :] = jnp.zeros((8, COLS), jnp.float32)
        spread[pl.ds(0, small.shape[0]), 0:ROWS] = small.astype(jnp.float32)
        return spread[pl.ds(0, 8), :].T[:ROWS]

    face = upright(face_in[...])
    idx = upright(idx_in[...])
    weight = upright(weight_in[...])
    offs[pl.ds(0, ROWS), :] = jnp.broadcast_to(face[:, 0:1], (ROWS, COLS))
    offs[pl.ds(ROWS, ROWS), :] = jnp.broadcast_to(face[:, 1:2], (ROWS, COLS))
    cell = lanes(ROWS).astype(jnp.float32)
    spread[...] = jnp.zeros_like(spread)
    for side in range(2):
        total = jnp.zeros((ROWS, 1), jnp.float32)
        values = jnp.zeros((ROWS, COLS), jnp.float32)
        for j in range(4):
            c = side * 4 + j
            w = weight[:, c : c + 1]
            total = total + w
            values = values + jnp.where(idx[:, c : c + 1] == cell, w, 0.0)
        spread[pl.ds(side * EXT + HALO, ROWS), :] = values / total
    for side in range(2):
        for yb in range(YB):
            table[pl.ds(side * EXT + yb * YC, YC), :] = spread[pl.ds(side * EXT + yb, YC, stride=YB), :]


def open_kernel(sc, own, got1, got2, got3, table, offs, ends, og, swap, chosen):
    swap[pl.ds(SHARE, 2 * ROWS), :] = offs[...]
    swap[pl.ds(SHARE + 2 * ROWS, 2 * ROWS), :] = ends[pl.ds(YB * SHARE, 2 * ROWS), :]
    for yb in range(YB):
        og[pl.ds(yb * SHARE, 64), :] = ends[pl.ds(yb * SHARE, 64), :]
        og[pl.ds(yb * SHARE + 96, 8), :] = ends[pl.ds(yb * SHARE + 96, 8), :]
    pbx = sc[S_PBX]
    value = own[...]
    for code, got in ((1, got1), (2, got2), (3, got3)):
        value = jnp.where(pbx == code, got[...], value)
    chosen[...] = value
    rows = []
    for f in range(FIELDS):
        for kb in range(KB):
            for a in range(2):
                rows.append(chosen[pl.ds(f * LEVELS + kb + a * 8 * KB, 8, stride=KB), :])
    weights = jnp.concatenate([table[...], jnp.zeros((COLS - 2 * EXT, COLS), jnp.float32)], axis=0)
    values = lax.dot_general(
        jnp.concatenate(rows, axis=0), weights, (((1,), (1,)), ((), ())),
        precision=HIGHEST, preferred_element_type=jnp.float32,
    )
    shift = (lanes() // KA - sublanes()) % 8
    for half in range(2):
        upright = values[half * COLS : (half + 1) * COLS].T
        for i in range(2 * YB):
            part = upright[i * YC : (i + 1) * YC]
            value = part
            for d in range(1, 8):
                value = jnp.where(shift == d, pltpu.roll(pltpu.roll(part, KA * d, 1), 8 - d, 0), value)
            og[pl.ds((i % YB) * SHARE + 64 + (i // YB) * 16 + half * 8, 8), :] = value
    chunk = lanes(SHARE) // KA
    planes = [og[pl.ds(yb * SHARE, SHARE), :] for yb in range(YB)]
    swap[pl.ds(0, SHARE), :] = jnp.where(
        chunk % 4 == 3, pltpu.roll(planes[0], KA, 1),
        jnp.where(chunk % 4 == 0, pltpu.roll(planes[2], COLS - KA, 1), planes[1]),
    )


def columns_of(state, edges):
    for c, x in enumerate((COLS - 1, 0, COLS - 2, 1)):
        for i in range(BLOCKS // 8):
            edges[pl.ds(c * BLOCKS + 8 * i, 8), :] = state[pl.ds(PAD + 8 * i * COLS + x, 8, stride=COLS), :]


def halos(sc, one, two):
    even = sc[S_EVEN] == 1
    top = jnp.where(sc[S_TOP] == 1, jnp.where(even, two, one), 0.0)
    bottom = jnp.where(sc[S_BOTTOM] == 1, jnp.where(even, one, two), 0.0)
    return top, bottom


def turn_kernel(sc, nest, wide1, wide2, edge1, edge2, far_mask, far_mixing, state, coef, ext, mask, mixing, sems):
    copies = [
        pltpu.make_async_copy(far_mask, mask, sems.at[0]),
        pltpu.make_async_copy(far_mixing, mixing, sems.at[1]),
    ]
    for copy in copies:
        copy.start()
    pad = jnp.zeros((PAD, COLS), jnp.float32)
    state[pl.ds(0, PAD), :] = pad
    state[pl.ds(STATE_ROWS - PAD, PAD), :] = pad
    even = sc[S_EVEN] == 1
    top_in, bottom_in = sc[S_TOP] == 1, sc[S_BOTTOM] == 1
    for yb in range(YB):

        def tile(i, yb=yb):
            base = (i // KB) * LEVELS + i % KB
            rows = []
            for yc in range(YC):
                r = YB * yc + yb
                for a in range(2):
                    level = base + a * 8 * KB
                    if HALO <= r < HALO + ROWS:
                        rows.append(nest[pl.ds(level * ROWS + r - HALO, 8, stride=KB * ROWS), :])
                    else:
                        at = pl.ds(level * HALO + r % ROWS % HALO, 8, stride=KB * HALO)
                        one, two = wide1[at, :], wide2[at, :]
                        if r < HALO:
                            rows.append(jnp.where(top_in, jnp.where(even, two, one), 0.0))
                        else:
                            rows.append(jnp.where(bottom_in, jnp.where(even, one, two), 0.0))
            at = pl.multiple_of(PAD + (yb * 16 + i) * COLS, 8)
            state[pl.ds(at, COLS), :] = jnp.concatenate(rows, axis=0).T

        unrolled(16, TILES, tile)
    for copy in copies:
        copy.wait()
    for i, plane in enumerate((mask[...].astype(jnp.float32), mixing[...])):
        at = SHARE + (2 + i) * ROWS
        low, high = pl.ds(at, HALO), pl.ds(at + ROWS - HALO, HALO)
        top = halos(sc, edge1[high, :], edge2[high, :])[0]
        bottom = halos(sc, edge1[low, :], edge2[low, :])[1]
        ext[pl.ds(i * EXT, HALO), :] = top
        ext[pl.ds(i * EXT + HALO, ROWS), :] = plane
        ext[pl.ds(i * EXT + HALO + ROWS, HALO), :] = bottom
    for yb in range(YB):
        for i in range(2):
            rows = [
                jnp.broadcast_to(ext[pl.ds(i * EXT + YB * yc + yb, 1), :], (KA, COLS)) for yc in range(YC)
            ]
            coef[pl.ds((i * YB + yb) * COLS, COLS), :] = jnp.concatenate(rows, axis=0).T


def message_kernel(sc, og, offs, edge1, edge2, ogx, offv, edges, msg_e, msg_o, msg_lo, msg_hi, left, right, ext, joint):
    mine = sublanes() == lanes() // KA
    even = sc[S_EVEN] == 1
    for i in range(2):
        at = SHARE + i * ROWS
        one_low, one_high = edge1[pl.ds(at, HALO), :], edge1[pl.ds(at + ROWS - HALO, HALO), :]
        two_low, two_high = edge2[pl.ds(at, HALO), :], edge2[pl.ds(at + ROWS - HALO, HALO), :]
        ext[pl.ds(i * EXT, HALO), :] = jnp.where(even, two_high, one_high)
        ext[pl.ds(i * EXT + HALO, ROWS), :] = offs[pl.ds(i * ROWS, ROWS), :]
        ext[pl.ds(i * EXT + HALO + ROWS, HALO), :] = jnp.where(even, one_low, two_low)
        for yb in range(YB):
            away = ext[pl.ds(i * EXT + yb, YC, stride=YB), :]
            offv[pl.ds(i * YB + yb, 1), :] = jnp.sum(jnp.where(mine, away, 0.0), axis=0, keepdims=True)
    chunk = lanes(SHARE) // KA
    top, bottom = halos(sc, edge1[pl.ds(0, SHARE), :], edge2[pl.ds(0, SHARE), :])
    for yb in range(YB):
        rows = pl.ds(yb * SHARE, SHARE)
        row = YB * chunk + yb
        up = pltpu.roll(top, KA * (3, 4, 1)[yb], 1)
        down = pltpu.roll(bottom, KA * (7, 4, 5)[yb], 1)
        joint[rows, :] = jnp.where(row < HALO, up, jnp.where(row >= HALO + ROWS, down, og[rows, :]))
        for c in range(4):
            edges[pl.ds(c * BLOCKS + yb * 16, 16), :] = joint[pl.ds(yb * SHARE + c * 16, 16), :]
        for side in range(2):
            ogx[pl.ds(side * BLOCKS + yb * 16, 16), :] = joint[pl.ds(yb * SHARE + 64 + side * 16, 16), :]
    number = sc[S_PB].astype(jnp.float32)
    for ref, third, opened, fact, off in ((right, 2, 1, 0, 1), (left, 3, 0, 2, 0)):
        ref[pl.ds(0, 2 * BLOCKS), :] = edges[pl.ds(0, 2 * BLOCKS), :]
        ref[pl.ds(2 * BLOCKS, BLOCKS), :] = edges[pl.ds(third * BLOCKS, BLOCKS), :]
        ref[pl.ds(3 * BLOCKS, BLOCKS), :] = ogx[pl.ds(opened * BLOCKS, BLOCKS), :]
        ref[pl.ds(4 * BLOCKS, 16), :] = jnp.zeros((16, COLS), jnp.float32) + number
        for yb in range(YB):
            for i in range(2):
                ref[pl.ds(4 * BLOCKS + i * YB + yb, 1), :] = joint[pl.ds(yb * SHARE + 96 + fact + i, 1), :]
        ref[pl.ds(4 * BLOCKS + 2 * YB, YB), :] = offv[pl.ds(off * YB, YB), :]
    x_even, low = sc[S_XEVEN] == 1, sc[S_LOW] == 1
    msg_e[...] = jnp.where(x_even, right[...], left[...])
    msg_o[...] = jnp.where(x_even, left[...], right[...])
    msg_lo[...] = jnp.where(low, right[...], left[...])
    msg_hi[...] = jnp.where(low, left[...], right[...])


def coefficients(wet, mix):
    kmix = wet * mix
    return kmix, wet - 4.0 * TIME_STEP * wet - 2.0 * kmix, TIME_STEP * wet, TURN * wet


def advance_edge(q, east, west, wet, mix):
    sub, lane = sublanes(), lanes() % KA
    new = []
    for yb in range(YB):
        kmix, centre, base, turn = coefficients(wide(wet[yb]), wide(mix[yb]))
        flow = q[yb][1]
        swapped = pltpu.roll(flow, 4, 0)
        cu = turn * jnp.where(sub < 4, flow, swapped)
        cv = turn * jnp.where(sub < 4, swapped, flow)
        pair = []
        for half in range(2):
            c = q[yb][half]
            above = jnp.where(
                sub % KB >= 1, pltpu.roll(c, 1, 0),
                jnp.where(lane == 0, c, pltpu.roll(pltpu.roll(c, 5, 0), 1, 1)),
            )
            below = jnp.where(
                sub % KB < KB - 1, pltpu.roll(c, 7, 0),
                jnp.where(lane == KA - 1, c, pltpu.roll(pltpu.roll(c, 3, 0), COLS - 1, 1)),
            )
            south = q[yb - 1][half] if yb > 0 else pltpu.roll(q[YB - 1][half], KA, 1)
            north = q[yb + 1][half] if yb < YB - 1 else pltpu.roll(q[0][half], COLS - KA, 1)
            value = (centre * c + (base - cu) * east[yb][half]) + ((base + cu) * west[yb][half] + (base - cv) * north)
            value = value + ((base + cv) * south + kmix * (above + below))
            if half == 1:
                value = value + jnp.where(sub < 4, cv, -cu)
            pair.append(value)
        new.append(pair)
    return new


def ghosts(side, ogx, offv, west0, east0, west1, east1):
    def column(slot, c):
        return [
            [side[pl.ds(slot * SIDE_ROWS + c * BLOCKS + yb * 16 + half * 8, 8), :] for half in range(2)]
            for yb in range(YB)
        ]

    def fact(slot, i):
        return [side[pl.ds(slot * SIDE_ROWS + 4 * BLOCKS + i * YB + yb, 1), :] for yb in range(YB)]

    def pick(away, choices, value):
        for e, choice in choices:
            value = [
                [jnp.where(wide(away[yb]) == e, choice[yb][half], value[yb][half]) for half in range(2)]
                for yb in range(YB)
            ]
        return value

    def put(ref, value):
        for yb in range(YB):
            for half in range(2):
                ref[pl.ds(yb * 16 + half * 8, 8), :] = value[yb][half]

    for sign, first, second in ((-1, west0, west1), (1, east0, east1)):
        which = 0 if sign < 0 else 1
        away = [offv[pl.ds(which * YB + yb, 1), :] for yb in range(YB)]
        opened = [
            [ogx[pl.ds(which * BLOCKS + yb * 16 + half * 8, 8), :] for half in range(2)] for yb in range(YB)
        ]
        reach = range(1, REACH + 1)
        put(first, pick(away, [(d, column(REACH + sign * d, which)) for d in reach], opened))
        later = opened
        for d in reach:
            slot = REACH + sign * d
            outer = pick(
                fact(slot, 2), [(e, column(slot - sign * e, 1 - which)) for e in reach], column(slot, 3)
            )
            inner = column(slot, 2)
            east, west = (outer, inner) if sign < 0 else (inner, outer)
            new = advance_edge(column(slot, which), east, west, fact(slot, 0), fact(slot, 1))
            later = pick(away, [(d, new)], later)
        put(second, later)


def substep(src, dst, west_ghost, east_ghost, coef):
    sub, ka = sublanes(), lanes() % KA

    def block(yb, f, kb):
        return (yb * FIELDS + f) * KB + kb

    for yb in range(YB):

        def group(xg, first, last, yb=yb):
            x = xg * 8

            def load(yb, f, kb, shift=0):
                return src[pl.ds(PAD + block(yb, f, kb) * COLS + x + shift, 8), :]

            kmix, centre, base, turn = coefficients(
                coef[pl.ds(yb * COLS + x, 8), :], coef[pl.ds((YB + yb) * COLS + x, 8), :]
            )
            q = [[load(yb, f, kb) for kb in range(KB)] for f in range(FIELDS)]
            for kb in range(KB):
                cu, cv = turn * q[2][kb], turn * q[3][kb]
                ke, kw, kn, ks = base - cu, base + cu, base - cv, base + cv
                for f in range(FIELDS):
                    c = q[f][kb]
                    b = block(yb, f, kb)
                    west, east = load(yb, f, kb, -1), load(yb, f, kb, 1)
                    if first:
                        west = jnp.where(sub == 0, wide(west_ghost[pl.ds(b, 1), :]), west)
                    if last:
                        east = jnp.where(sub == 7, wide(east_ghost[pl.ds(b, 1), :]), east)
                    south = load(yb - 1, f, kb) if yb > 0 else pltpu.roll(load(YB - 1, f, kb), KA, 1)
                    north = load(yb + 1, f, kb) if yb < YB - 1 else pltpu.roll(load(0, f, kb), COLS - KA, 1)
                    above = q[f][kb - 1] if kb > 0 else jnp.where(ka == 0, c, pltpu.roll(q[f][KB - 1], 1, 1))
                    below = q[f][kb + 1] if kb < KB - 1 else jnp.where(ka == KA - 1, c, pltpu.roll(q[f][0], COLS - 1, 1))
                    new = (centre * c + ke * east) + (kw * west + kn * north)
                    new = new + (ks * south + kmix * (above + below))
                    if f == 2:
                        new = new + cv
                    if f == 3:
                        new = new - cu
                    dst[pl.ds(PAD + b * COLS + x, 8), :] = new

        group(0, True, False)

        def body(i, carry, group=group):
            for j in range(UNROLL):
                group(1 + i * UNROLL + j, False, False)
            return carry

        lax.fori_loop(0, (COLS // 8 - 2) // UNROLL, body, 0)
        group(COLS // 8 - 1, False, True)


UNROLL = 2
TILES = 4


def clear_pads(*refs):
    for ref in refs:
        ref[pl.ds(0, PAD), :] = jnp.zeros((PAD, COLS), jnp.float32)
        ref[pl.ds(STATE_ROWS - PAD, PAD), :] = jnp.zeros((PAD, COLS), jnp.float32)


def first_kernel(
    sc, state, own, ogx, coef, offv, r0, r1, r2, r3, r4, r5, out, edges, side, mid, west0, east0, west1, east1
):
    clear_pads(mid, out)
    side[pl.ds(REACH * SIDE_ROWS, 2 * BLOCKS), :] = own[pl.ds(0, 2 * BLOCKS), :]
    for j, r in enumerate((r0, r1, r2, r3, r4, r5)):
        side[pl.ds(pl.multiple_of(sc[S_SLOT + j] * SIDE_ROWS, 8), SIDE_ROWS), :] = r[...]
    ghosts(side, ogx, offv, west0, east0, west1, east1)
    substep(state, mid, west0, east0, coef)
    substep(mid, out, west1, east1, coef)
    columns_of(out, edges)


def second_kernel(
    sc, state, own, ogx, coef, offv, r0, r1, r2, r3, r4, r5, s0, s1, s2, s3, s4, s5,
    out, means, blocks, side, mid, west0, east0, west1, east1, end, nat, sems,
):
    clear_pads(mid)
    side[pl.ds(REACH * SIDE_ROWS, 2 * BLOCKS), :] = own[pl.ds(0, 2 * BLOCKS), :]
    for j, (r, s) in enumerate(zip((r0, r1, r2, r3, r4, r5), (s0, s1, s2, s3, s4, s5))):
        slot = sc[S_SLOT + j]
        at = slot * SIDE_ROWS
        third = pl.multiple_of(jnp.where(slot > REACH, 3 * BLOCKS, 2 * BLOCKS), 8)
        side[pl.ds(pl.multiple_of(at, 8), 2 * BLOCKS), :] = s[pl.ds(0, 2 * BLOCKS), :]
        side[pl.ds(pl.multiple_of(at + 2 * BLOCKS, 8), BLOCKS), :] = s[pl.ds(third, BLOCKS), :]
        side[pl.ds(pl.multiple_of(at + 3 * BLOCKS, 8), BLOCKS + 16), :] = r[pl.ds(3 * BLOCKS, BLOCKS + 16), :]
    ghosts(side, ogx, offv, west0, east0, west1, east1)
    substep(state, mid, west0, east0, coef)
    substep(mid, end, west1, east1, coef)
    for j in range(3):
        blocks[pl.ds(j * 8, 8), :] = wide((r0, r1, r2)[j][pl.ds(SIDE_ROWS - 1, 1), :])
    share = LEVELS * ROWS
    copies = [
        pltpu.make_async_copy(nat.at[pl.ds(f * share, share)], out.at[pl.ds(f * share, share)], sems.at[f])
        for f in range(FIELDS)
    ]
    for f in range(FIELDS):
        for yb in range(YB):

            def tile(kb, yb=yb, f=f):
                base = f * LEVELS + kb
                block = (yb * FIELDS + f) * KB + kb
                rows = end[pl.ds(pl.multiple_of(PAD + block * COLS, 8), COLS), :].T
                for yc in range(YC):
                    r = YB * yc + yb - HALO
                    if 0 <= r < ROWS:
                        for a in range(2):
                            at = pl.ds((base + a * 8 * KB) * ROWS + r, 8, stride=KB * ROWS)
                            nat[at, :] = rows[yc * KA + 8 * a : yc * KA + 8 * a + 8]

            unrolled(KB, TILES, tile)
        copies[f].start()

    target = lanes(COLS)
    block = 64
    for b in range(FIELDS * LEVELS // block):
        total = jnp.zeros((block, COLS), jnp.float32)
        for a in range(4):
            rows = []
            for c in range(block // 8):
                at = (b * block + c * 8) * ROWS + 4 * a
                part = [nat[pl.ds(at + i, 8, stride=ROWS), :] for i in range(4)]
                rows.append((part[0] + part[1]) + (part[2] + part[3]))
            gather = jnp.where(a * 32 + sublanes(COLS) // 4 == target, 1.0 / 16.0, 0.0).astype(jnp.float32)
            total = total + lax.dot_general(
                jnp.concatenate(rows, axis=0), gather, (((1,), (0,)), ((), ())),
                precision=HIGHEST, preferred_element_type=jnp.float32,
            )
        means[pl.ds(b * block, block), :] = total
    for copy in copies:
        copy.wait()


def feedback_kernel(sc, coarse, means, got1, got2, got3, blocks, out):
    me = sc[S_ME].astype(jnp.float32)
    for i in range(FIELDS * LEVELS // 8):
        rows = pl.ds(i * 8, 8)
        value = means[rows, :]
        for j, got in enumerate((got1, got2, got3)):
            value = jnp.where(blocks[pl.ds(j * 8, 8), :] == me, got[rows, :], value)
        old = coarse[rows, :]
        out[rows, :] = old + FEEDBACK * (value - old)


def call(kernel, outs, scratch, *args, far=(), far_out=(), cost=None):
    def spec(i, places, arg=None):
        if i in places:
            return pl.BlockSpec(memory_space=pltpu.HBM)
        small = arg is not None and arg.ndim == 1
        return pl.BlockSpec(memory_space=pltpu.SMEM if small else pltpu.VMEM)

    return pl.pallas_call(
        kernel,
        out_shape=[jax.ShapeDtypeStruct(s, jnp.float32) for s in outs],
        in_specs=[spec(i, far, a) for i, a in enumerate(args)],
        out_specs=[spec(i, far_out) for i in range(len(outs))],
        scratch_shapes=[pltpu.VMEM(s, jnp.float32) if isinstance(s, tuple) else s for s in scratch],
        cost_estimate=None if cost is None else pl.CostEstimate(flops=cost, bytes_accessed=cost, transcendentals=0),
        compiler_params=pltpu.CompilerParams(vmem_limit_bytes=VMEM_BYTES),
    )(*args)


def per_device(nest_state, mixing, land_mask, face_off, parent_state, parent_block, interp_idx, interp_w):
    tiles = lax.axis_size("nest")
    blocks = lax.axis_size("parent")
    n = lax.axis_index("nest")
    p = lax.axis_index("parent")
    x = n % GROUP
    own_block = parent_block[0, 0]

    def inside(code):
        return [(s, s ^ code) for s in range(tiles)]

    def across(pairs):
        links = []
        for g in range(tiles // GROUP):
            for a, b in pairs:
                i, j = GROUP * g + a, (GROUP * (g + 1) + b) % tiles
                links += [(i, j), (j, i)]
        return links

    rows_1 = [(s, s ^ 1) for s in range(blocks)]
    rows_2 = [(s, ((s + 1) ^ 1) - 1) if 0 < s < blocks - 1 else (s, blocks - 1 - s) for s in range(blocks)]
    links = [
        inside(1), inside(2), inside(3),
        across([(3, 0), (2, 1)]), across([(3, 1), (2, 0)]), across([(3, 2), (1, 0)]),
    ]
    x_even, low = x % 2 == 0, x < 2
    rel = [
        jnp.where(x_even, 1, -1),
        jnp.where(low, 2, -2),
        3 - 2 * x,
        jnp.where(low, -1 - 2 * x, 7 - 2 * x),
        jnp.where(low, -2, 2),
        jnp.where(x_even, -3, 3),
    ]
    sc = jnp.stack(
        [
            (p % 2 == 0).astype(jnp.int32),
            (p > 0).astype(jnp.int32),
            (p < blocks - 1).astype(jnp.int32),
            own_block ^ n,
        ]
        + [REACH + r for r in rel]
        + [x_even.astype(jnp.int32), low.astype(jnp.int32), own_block, n]
    ).astype(jnp.int32)

    nest2 = nest_state.reshape(FIELDS * LEVELS * ROWS, COLS)
    coarse = parent_state.reshape(FIELDS * LEVELS, COLS)
    natural = (FIELDS * LEVELS * ROWS, COLS)
    rows, narrow = (WIDE_ROWS, COLS), (ROWS, COLS)
    got = [lax.ppermute(coarse, "nest", links[i]) for i in range(3)]
    pay1, pay2 = call(rows_kernel, [rows, rows], [], sc, nest2)
    (ends,) = call(
        ends_kernel, [(YB * SHARE + 2 * ROWS, COLS)], [(2 * EXT, COLS)], nest2, land_mask, mixing, cost=SMALL
    )
    wide1 = lax.ppermute(pay1, "parent", rows_1)
    wide2 = lax.ppermute(pay2, "parent", rows_2)
    face, idx, weight = (
        face_off.T, interp_idx.transpose(1, 2, 0).reshape(8, ROWS), interp_w.transpose(1, 2, 0).reshape(8, ROWS)
    )
    coarse_rows = (FIELDS * LEVELS, COLS)
    table, offs, kept = call(
        table_kernel, [(2 * EXT, COLS), (2 * ROWS, COLS), coarse_rows],
        [(2 * EXT, COLS), coarse_rows, pltpu.VMEM((2, ROWS), jnp.int32), pltpu.VMEM((8, ROWS), jnp.int32),
         pltpu.VMEM((8, ROWS), jnp.float32), pltpu.SemaphoreType.DMA((4,))],
        coarse, face, idx, weight, far=(0, 1, 2, 3), cost=SMALL,
    )
    block, state_rows = (BLOCKS, COLS), (STATE_ROWS, COLS)
    og, swap = call(
        open_kernel, [(YB * SHARE, COLS), (SWAP_ROWS, COLS)], [coarse_rows], sc, kept, *got, table, offs, ends
    )
    edge1 = lax.ppermute(swap, "parent", rows_1)
    edge2 = lax.ppermute(swap, "parent", rows_2)
    side = (SIDE_ROWS, COLS)
    ogx, offv, edges, msg_e, msg_o, msg_lo, msg_hi = call(
        message_kernel, [(2 * BLOCKS, COLS), (8, COLS), (4 * BLOCKS, COLS)] + [side] * 4,
        [side, side, (2 * EXT, COLS), (YB * SHARE, COLS)], sc, og, offs, edge1, edge2,
    )
    nest_later, offv = lax.optimization_barrier((nest2, offv))
    state, coef = call(
        turn_kernel, [state_rows, (2 * YB * COLS, COLS)],
        [(2 * EXT, COLS), pltpu.VMEM(narrow, jnp.int32), pltpu.VMEM(narrow, jnp.float32), pltpu.SemaphoreType.DMA((2,))],
        sc, nest_later, wide1, wide2, edge1, edge2, land_mask, mixing, far=(6, 7),
    )
    msgs = [msg_e, msg_lo, msg_lo, msg_hi, msg_hi, msg_o]
    first = [lax.ppermute(m, "nest", link) for m, link in zip(msgs, links)]
    work = [(SLOTS * SIDE_ROWS, COLS), state_rows] + [block] * 4
    state, edges = call(
        first_kernel, [state_rows, (4 * BLOCKS, COLS)], work, sc, state, edges, ogx, coef, offv, *first
    )
    second = [lax.ppermute(edges, "nest", link) for link in links]
    new2, means, blocks = call(
        second_kernel, [natural, coarse_rows, (24, COLS)],
        work + [state_rows, natural, pltpu.SemaphoreType.DMA((FIELDS,))],
        sc, state, edges, ogx, coef, offv, *first, *second, far_out=(0,),
    )
    arrived = [lax.ppermute(means, "nest", links[i]) for i in range(3)]
    (parent_new,) = call(feedback_kernel, [coarse_rows], [], sc, kept, means, *arrived, blocks)
    return new2.reshape(nest_state.shape), parent_new.reshape(parent_state.shape)


def solution(mesh):
    return jax.shard_map(
        per_device,
        mesh=mesh,
        in_specs=(
            P(None, None, "parent", "nest"),
            P("parent", "nest"),
            P("parent", "nest"),
            P("parent", "nest"),
            P(None, None, "parent", "nest"),
            P("parent", "nest"),
            P("parent", "nest", None),
            P("parent", "nest", None),
        ),
        out_specs=(P(None, None, "parent", "nest"), P(None, None, "parent", "nest")),
        check_vma=False,
    )
```

```python
import jax
import jax.numpy as jnp
from jax import lax
from jax.experimental import pallas as pl
from jax.experimental.pallas import tpu as pltpu
from jax.sharding import PartitionSpec as P

FIELDS = 4
LEVELS = 64
ROWS = 16
COLS = 128
HALO = 4
EXT = ROWS + 2 * HALO
YB = 3
YC = 8
KB = 4
KA = 16
BLOCKS = YB * FIELDS * KB
PAD = 8
STATE_ROWS = BLOCKS * COLS + 2 * PAD
SIDE_ROWS = 4 * BLOCKS + 16
MESSAGE_ROWS = 6 * BLOCKS + 32
SHARE = 6 * 16 + 8
SWAP_ROWS = SHARE + 4 * ROWS
WIDE_ROWS = FIELDS * LEVELS * HALO
REACH = 3
SMALL = 1000
SLOTS = 2 * REACH + 1
GROUP = 4
VMEM_BYTES = 44 * 1024 * 1024

TIME_STEP = 0.1
TURN = 0.05
FEEDBACK = 0.5
HIGHEST = lax.Precision.HIGHEST

S_EVEN, S_TOP, S_BOTTOM, S_PBX, S_SLOT, S_XEVEN, S_LOW, S_PB, S_ME = 0, 1, 2, 3, 4, 10, 11, 12, 13


def lanes(rows=8):
    return lax.broadcasted_iota(jnp.int32, (rows, COLS), 1)


def sublanes(rows=8):
    return lax.broadcasted_iota(jnp.int32, (rows, COLS), 0)


def wide(row):
    return jnp.broadcast_to(row, (8, COLS))


def unrolled(count, step, body):
    def several(i, carry):
        for j in range(step):
            body(i * step + j)
        return carry

    lax.fori_loop(0, count // step, several, 0)


def rows_kernel(sc, nest, pay1, pay2):
    even = sc[S_EVEN] == 1
    first = jnp.where(even, ROWS - HALO, 0)
    second = jnp.where(even, 0, ROWS - HALO)

    def move(i):
        at, to = i * ROWS, i * HALO
        pay1[pl.ds(to, HALO), :] = nest[pl.ds(at + first, HALO), :]
        pay2[pl.ds(to, HALO), :] = nest[pl.ds(at + second, HALO), :]

    unrolled(FIELDS * LEVELS, 16, move)


def ends_kernel(nest, mask, mixing, ends, ext):
    nothing = jnp.zeros((8, COLS), jnp.float32)
    ext[...] = jnp.zeros_like(ext)
    planes = (mask[...].astype(jnp.float32), mixing[...])
    for i, plane in enumerate(planes):
        ext[pl.ds(i * EXT + HALO, ROWS), :] = plane
        ends[pl.ds(YB * SHARE + i * ROWS, ROWS), :] = plane
    for yb in range(YB):
        ends[pl.ds(yb * SHARE + 96, 8), :] = nothing
        for i in range(2):
            rows = [jnp.broadcast_to(ext[pl.ds(i * EXT + YB * yc + yb, 1), :], (KA, COLS)) for yc in range(YC)]
            tile = jnp.concatenate(rows, axis=0).T
            ends[pl.ds(yb * SHARE + 96 + i, 1), :] = tile[COLS - 1 : COLS]
            ends[pl.ds(yb * SHARE + 98 + i, 1), :] = tile[0:1]

        def take(i, yb=yb):
            base = (i // KB) * LEVELS + i % KB
            rows = []
            for yc in range(YC):
                r = YB * yc + yb - HALO
                for a in range(2):
                    if 0 <= r < ROWS:
                        rows.append(nest[pl.ds((base + a * 8 * KB) * ROWS + r, 8, stride=KB * ROWS), :])
                    else:
                        rows.append(nothing)
            tile = jnp.concatenate(rows, axis=0).T
            for c, x in enumerate((COLS - 1, 0, COLS - 2, 1)):
                ends[pl.ds(yb * SHARE + c * 16 + i, 1), :] = tile[x : x + 1]

        unrolled(16, TILES, take)


def table_kernel(coarse, face, idx, weight, table, offs, kept, spread, near, face_in, idx_in, weight_in, sems):
    pairs = ((coarse, near), (face, face_in), (idx, idx_in), (weight, weight_in))
    copies = [pltpu.make_async_copy(far, here, sems.at[i]) for i, (far, here) in enumerate(pairs)]
    for copy in copies:
        copy.start()
    for copy in copies:
        copy.wait()
    kept[...] = near[...]

    def upright(small):
        spread[pl.ds(0, 8), :] = jnp.zeros((8, COLS), jnp.float32)
        spread[pl.ds(0, small.shape[0]), 0:ROWS] = small.astype(jnp.float32)
        return spread[pl.ds(0, 8), :].T[:ROWS]

    face = upright(face_in[...])
    idx = upright(idx_in[...])
    weight = upright(weight_in[...])
    offs[pl.ds(0, ROWS), :] = jnp.broadcast_to(face[:, 0:1], (ROWS, COLS))
    offs[pl.ds(ROWS, ROWS), :] = jnp.broadcast_to(face[:, 1:2], (ROWS, COLS))
    cell = lanes(ROWS).astype(jnp.float32)
    spread[...] = jnp.zeros_like(spread)
    for side in range(2):
        total = jnp.zeros((ROWS, 1), jnp.float32)
        values = jnp.zeros((ROWS, COLS), jnp.float32)
        for j in range(4):
            c = side * 4 + j
            w = weight[:, c : c + 1]
            total = total + w
            values = values + jnp.where(idx[:, c : c + 1] == cell, w, 0.0)
        spread[pl.ds(side * EXT + HALO, ROWS), :] = values / total
    for side in range(2):
        for yb in range(YB):
            table[pl.ds(side * EXT + yb * YC, YC), :] = spread[pl.ds(side * EXT + yb, YC, stride=YB), :]


def open_kernel(sc, own, got1, got2, got3, table, offs, ends, og, swap, chosen):
    swap[pl.ds(SHARE, 2 * ROWS), :] = offs[...]
    swap[pl.ds(SHARE + 2 * ROWS, 2 * ROWS), :] = ends[pl.ds(YB * SHARE, 2 * ROWS), :]
    for yb in range(YB):
        og[pl.ds(yb * SHARE, 64), :] = ends[pl.ds(yb * SHARE, 64), :]
        og[pl.ds(yb * SHARE + 96, 8), :] = ends[pl.ds(yb * SHARE + 96, 8), :]
    pbx = sc[S_PBX]
    value = own[...]
    for code, got in ((1, got1), (2, got2), (3, got3)):
        value = jnp.where(pbx == code, got[...], value)
    chosen[...] = value
    rows = []
    for f in range(FIELDS):
        for kb in range(KB):
            for a in range(2):
                rows.append(chosen[pl.ds(f * LEVELS + kb + a * 8 * KB, 8, stride=KB), :])
    weights = jnp.concatenate([table[...], jnp.zeros((COLS - 2 * EXT, COLS), jnp.float32)], axis=0)
    values = lax.dot_general(
        jnp.concatenate(rows, axis=0), weights, (((1,), (1,)), ((), ())),
        precision=HIGHEST, preferred_element_type=jnp.float32,
    )
    shift = (lanes() // KA - sublanes()) % 8
    for half in range(2):
        upright = values[half * COLS : (half + 1) * COLS].T
        for i in range(2 * YB):
            part = upright[i * YC : (i + 1) * YC]
            value = part
            for d in range(1, 8):
                value = jnp.where(shift == d, pltpu.roll(pltpu.roll(part, KA * d, 1), 8 - d, 0), value)
            og[pl.ds((i % YB) * SHARE + 64 + (i // YB) * 16 + half * 8, 8), :] = value
    chunk = lanes(SHARE) // KA
    planes = [og[pl.ds(yb * SHARE, SHARE), :] for yb in range(YB)]
    swap[pl.ds(0, SHARE), :] = jnp.where(
        chunk % 4 == 3, pltpu.roll(planes[0], KA, 1),
        jnp.where(chunk % 4 == 0, pltpu.roll(planes[2], COLS - KA, 1), planes[1]),
    )


def columns_of(state, edges):
    for c, x in enumerate((COLS - 1, 0, COLS - 2, 1)):
        for i in range(BLOCKS // 8):
            edges[pl.ds(c * BLOCKS + 8 * i, 8), :] = state[pl.ds(PAD + 8 * i * COLS + x, 8, stride=COLS), :]


def halos(sc, one, two):
    even = sc[S_EVEN] == 1
    top = jnp.where(sc[S_TOP] == 1, jnp.where(even, two, one), 0.0)
    bottom = jnp.where(sc[S_BOTTOM] == 1, jnp.where(even, one, two), 0.0)
    return top, bottom


def turn_kernel(sc, nest, wide1, wide2, edge1, edge2, far_mask, far_mixing, state, coef, ext, mask, mixing, sems):
    copies = [
        pltpu.make_async_copy(far_mask, mask, sems.at[0]),
        pltpu.make_async_copy(far_mixing, mixing, sems.at[1]),
    ]
    for copy in copies:
        copy.start()
    pad = jnp.zeros((PAD, COLS), jnp.float32)
    state[pl.ds(0, PAD), :] = pad
    state[pl.ds(STATE_ROWS - PAD, PAD), :] = pad
    even = sc[S_EVEN] == 1
    top_in, bottom_in = sc[S_TOP] == 1, sc[S_BOTTOM] == 1
    for yb in range(YB):

        def tile(i, yb=yb):
            base = (i // KB) * LEVELS + i % KB
            rows = []
            for yc in range(YC):
                r = YB * yc + yb
                for a in range(2):
                    level = base + a * 8 * KB
                    if HALO <= r < HALO + ROWS:
                        rows.append(nest[pl.ds(level * ROWS + r - HALO, 8, stride=KB * ROWS), :])
                    else:
                        at = pl.ds(level * HALO + r % ROWS % HALO, 8, stride=KB * HALO)
                        one, two = wide1[at, :], wide2[at, :]
                        if r < HALO:
                            rows.append(jnp.where(top_in, jnp.where(even, two, one), 0.0))
                        else:
                            rows.append(jnp.where(bottom_in, jnp.where(even, one, two), 0.0))
            at = pl.multiple_of(PAD + (yb * 16 + i) * COLS, 8)
            state[pl.ds(at, COLS), :] = jnp.concatenate(rows, axis=0).T

        unrolled(16, TILES, tile)
    for copy in copies:
        copy.wait()
    for i, plane in enumerate((mask[...].astype(jnp.float32), mixing[...])):
        at = SHARE + (2 + i) * ROWS
        low, high = pl.ds(at, HALO), pl.ds(at + ROWS - HALO, HALO)
        top = halos(sc, edge1[high, :], edge2[high, :])[0]
        bottom = halos(sc, edge1[low, :], edge2[low, :])[1]
        ext[pl.ds(i * EXT, HALO), :] = top
        ext[pl.ds(i * EXT + HALO, ROWS), :] = plane
        ext[pl.ds(i * EXT + HALO + ROWS, HALO), :] = bottom
    for yb in range(YB):
        for i in range(2):
            rows = [
                jnp.broadcast_to(ext[pl.ds(i * EXT + YB * yc + yb, 1), :], (KA, COLS)) for yc in range(YC)
            ]
            coef[pl.ds((i * YB + yb) * COLS, COLS), :] = jnp.concatenate(rows, axis=0).T


def message_kernel(sc, og, offs, edge1, edge2, ogx, offv, message, ext, joint):
    mine = sublanes() == lanes() // KA
    even = sc[S_EVEN] == 1
    for i in range(2):
        at = SHARE + i * ROWS
        one_low, one_high = edge1[pl.ds(at, HALO), :], edge1[pl.ds(at + ROWS - HALO, HALO), :]
        two_low, two_high = edge2[pl.ds(at, HALO), :], edge2[pl.ds(at + ROWS - HALO, HALO), :]
        ext[pl.ds(i * EXT, HALO), :] = jnp.where(even, two_high, one_high)
        ext[pl.ds(i * EXT + HALO, ROWS), :] = offs[pl.ds(i * ROWS, ROWS), :]
        ext[pl.ds(i * EXT + HALO + ROWS, HALO), :] = jnp.where(even, one_low, two_low)
        for yb in range(YB):
            away = ext[pl.ds(i * EXT + yb, YC, stride=YB), :]
            offv[pl.ds(i * YB + yb, 1), :] = jnp.sum(jnp.where(mine, away, 0.0), axis=0, keepdims=True)
    chunk = lanes(SHARE) // KA
    top, bottom = halos(sc, edge1[pl.ds(0, SHARE), :], edge2[pl.ds(0, SHARE), :])
    for yb in range(YB):
        rows = pl.ds(yb * SHARE, SHARE)
        row = YB * chunk + yb
        up = pltpu.roll(top, KA * (3, 4, 1)[yb], 1)
        down = pltpu.roll(bottom, KA * (7, 4, 5)[yb], 1)
        joint[rows, :] = jnp.where(row < HALO, up, jnp.where(row >= HALO + ROWS, down, og[rows, :]))
        for c in range(4):
            message[pl.ds(c * BLOCKS + yb * 16, 16), :] = joint[pl.ds(yb * SHARE + c * 16, 16), :]
        for side in range(2):
            ogx[pl.ds(side * BLOCKS + yb * 16, 16), :] = joint[pl.ds(yb * SHARE + 64 + side * 16, 16), :]
    number = sc[S_PB].astype(jnp.float32)
    message[pl.ds(4 * BLOCKS, BLOCKS), :] = ogx[pl.ds(BLOCKS, BLOCKS), :]
    message[pl.ds(5 * BLOCKS, BLOCKS), :] = ogx[pl.ds(0, BLOCKS), :]
    message[pl.ds(6 * BLOCKS, 32), :] = jnp.zeros((32, COLS), jnp.float32) + number
    for at, fact, off in ((6 * BLOCKS, 0, 1), (6 * BLOCKS + 16, 2, 0)):
        for yb in range(YB):
            for i in range(2):
                message[pl.ds(at + i * YB + yb, 1), :] = joint[pl.ds(yb * SHARE + 96 + fact + i, 1), :]
        message[pl.ds(at + 2 * YB, YB), :] = offv[pl.ds(off * YB, YB), :]


def coefficients(wet, mix):
    kmix = wet * mix
    return kmix, wet - 4.0 * TIME_STEP * wet - 2.0 * kmix, TIME_STEP * wet, TURN * wet


def advance_edge(q, east, west, wet, mix):
    sub, lane = sublanes(), lanes() % KA
    new = []
    for yb in range(YB):
        kmix, centre, base, turn = coefficients(wide(wet[yb]), wide(mix[yb]))
        flow = q[yb][1]
        swapped = pltpu.roll(flow, 4, 0)
        cu = turn * jnp.where(sub < 4, flow, swapped)
        cv = turn * jnp.where(sub < 4, swapped, flow)
        pair = []
        for half in range(2):
            c = q[yb][half]
            above = jnp.where(
                sub % KB >= 1, pltpu.roll(c, 1, 0),
                jnp.where(lane == 0, c, pltpu.roll(pltpu.roll(c, 5, 0), 1, 1)),
            )
            below = jnp.where(
                sub % KB < KB - 1, pltpu.roll(c, 7, 0),
                jnp.where(lane == KA - 1, c, pltpu.roll(pltpu.roll(c, 3, 0), COLS - 1, 1)),
            )
            south = q[yb - 1][half] if yb > 0 else pltpu.roll(q[YB - 1][half], KA, 1)
            north = q[yb + 1][half] if yb < YB - 1 else pltpu.roll(q[0][half], COLS - KA, 1)
            value = (centre * c + (base - cu) * east[yb][half]) + ((base + cu) * west[yb][half] + (base - cv) * north)
            value = value + ((base + cv) * south + kmix * (above + below))
            if half == 1:
                value = value + jnp.where(sub < 4, cv, -cu)
            pair.append(value)
        new.append(pair)
    return new


def ghosts(side, ogx, offv, west0, east0, west1, east1):
    def column(slot, c):
        return [
            [side[pl.ds(slot * SIDE_ROWS + c * BLOCKS + yb * 16 + half * 8, 8), :] for half in range(2)]
            for yb in range(YB)
        ]

    def fact(slot, i):
        return [side[pl.ds(slot * SIDE_ROWS + 4 * BLOCKS + i * YB + yb, 1), :] for yb in range(YB)]

    def pick(away, choices, value):
        for e, choice in choices:
            value = [
                [jnp.where(wide(away[yb]) == e, choice[yb][half], value[yb][half]) for half in range(2)]
                for yb in range(YB)
            ]
        return value

    def put(ref, value):
        for yb in range(YB):
            for half in range(2):
                ref[pl.ds(yb * 16 + half * 8, 8), :] = value[yb][half]

    for sign, first, second in ((-1, west0, west1), (1, east0, east1)):
        which = 0 if sign < 0 else 1
        away = [offv[pl.ds(which * YB + yb, 1), :] for yb in range(YB)]
        opened = [
            [ogx[pl.ds(which * BLOCKS + yb * 16 + half * 8, 8), :] for half in range(2)] for yb in range(YB)
        ]
        reach = range(1, REACH + 1)
        put(first, pick(away, [(d, column(REACH + sign * d, which)) for d in reach], opened))
        later = opened
        for d in reach:
            slot = REACH + sign * d
            outer = pick(
                fact(slot, 2), [(e, column(slot - sign * e, 1 - which)) for e in reach], column(slot, 3)
            )
            inner = column(slot, 2)
            east, west = (outer, inner) if sign < 0 else (inner, outer)
            new = advance_edge(column(slot, which), east, west, fact(slot, 0), fact(slot, 1))
            later = pick(away, [(d, new)], later)
        put(second, later)


def substep(src, dst, west_ghost, east_ghost, coef):
    sub, ka = sublanes(), lanes() % KA

    def block(yb, f, kb):
        return (yb * FIELDS + f) * KB + kb

    for yb in range(YB):

        def group(xg, first, last, yb=yb):
            x = xg * 8

            def load(yb, f, kb, shift=0):
                return src[pl.ds(PAD + block(yb, f, kb) * COLS + x + shift, 8), :]

            kmix, centre, base, turn = coefficients(
                coef[pl.ds(yb * COLS + x, 8), :], coef[pl.ds((YB + yb) * COLS + x, 8), :]
            )
            q = [[load(yb, f, kb) for kb in range(KB)] for f in range(FIELDS)]
            for kb in range(KB):
                cu, cv = turn * q[2][kb], turn * q[3][kb]
                ke, kw, kn, ks = base - cu, base + cu, base - cv, base + cv
                for f in range(FIELDS):
                    c = q[f][kb]
                    b = block(yb, f, kb)
                    west, east = load(yb, f, kb, -1), load(yb, f, kb, 1)
                    if first:
                        west = jnp.where(sub == 0, wide(west_ghost[pl.ds(b, 1), :]), west)
                    if last:
                        east = jnp.where(sub == 7, wide(east_ghost[pl.ds(b, 1), :]), east)
                    south = load(yb - 1, f, kb) if yb > 0 else pltpu.roll(load(YB - 1, f, kb), KA, 1)
                    north = load(yb + 1, f, kb) if yb < YB - 1 else pltpu.roll(load(0, f, kb), COLS - KA, 1)
                    above = q[f][kb - 1] if kb > 0 else jnp.where(ka == 0, c, pltpu.roll(q[f][KB - 1], 1, 1))
                    below = q[f][kb + 1] if kb < KB - 1 else jnp.where(ka == KA - 1, c, pltpu.roll(q[f][0], COLS - 1, 1))
                    new = (centre * c + ke * east) + (kw * west + kn * north)
                    new = new + (ks * south + kmix * (above + below))
                    if f == 2:
                        new = new + cv
                    if f == 3:
                        new = new - cu
                    dst[pl.ds(PAD + b * COLS + x, 8), :] = new

        group(0, True, False)

        def body(i, carry, group=group):
            for j in range(UNROLL):
                group(1 + i * UNROLL + j, False, False)
            return carry

        lax.fori_loop(0, (COLS // 8 - 2) // UNROLL, body, 0)
        group(COLS // 8 - 1, False, True)


UNROLL = 7
TILES = 4


def clear_pads(*refs):
    for ref in refs:
        ref[pl.ds(0, PAD), :] = jnp.zeros((PAD, COLS), jnp.float32)
        ref[pl.ds(STATE_ROWS - PAD, PAD), :] = jnp.zeros((PAD, COLS), jnp.float32)


def fill_sides(sc, side, own, columns, messages):
    side[pl.ds(REACH * SIDE_ROWS, 2 * BLOCKS), :] = own[pl.ds(0, 2 * BLOCKS), :]
    for j, (c, m) in enumerate(zip(columns, messages)):
        slot = sc[S_SLOT + j]
        east = slot > REACH
        parts = (
            (c, 0, 0, 2 * BLOCKS),
            (c, jnp.where(east, 3 * BLOCKS, 2 * BLOCKS), 2 * BLOCKS, BLOCKS),
            (m, jnp.where(east, 5 * BLOCKS, 4 * BLOCKS), 3 * BLOCKS, BLOCKS),
            (m, jnp.where(east, 6 * BLOCKS + 16, 6 * BLOCKS), 4 * BLOCKS, 16),
        )
        for ref, start, to, count in parts:
            at = pl.multiple_of(slot * SIDE_ROWS + to, 8)
            side[pl.ds(at, count), :] = ref[pl.ds(pl.multiple_of(start, 8), count), :]


def first_kernel(
    sc, state, own, ogx, coef, offv, r0, r1, r2, r3, r4, r5, out, edges, side, mid, west0, east0, west1, east1
):
    clear_pads(mid, out)
    received = (r0, r1, r2, r3, r4, r5)
    fill_sides(sc, side, own, received, received)
    ghosts(side, ogx, offv, west0, east0, west1, east1)
    substep(state, mid, west0, east0, coef)
    substep(mid, out, west1, east1, coef)
    columns_of(out, edges)


def second_kernel(
    sc, state, own, ogx, coef, offv, r0, r1, r2, r3, r4, r5, s0, s1, s2, s3, s4, s5,
    out, means, blocks, side, mid, west0, east0, west1, east1, end, nat, sems,
):
    clear_pads(mid)
    fill_sides(sc, side, own, (s0, s1, s2, s3, s4, s5), (r0, r1, r2, r3, r4, r5))
    ghosts(side, ogx, offv, west0, east0, west1, east1)
    substep(state, mid, west0, east0, coef)
    substep(mid, end, west1, east1, coef)
    for j in range(3):
        blocks[pl.ds(j * 8, 8), :] = wide((r0, r1, r2)[j][pl.ds(MESSAGE_ROWS - 1, 1), :])
    share = LEVELS * ROWS
    copies = [
        pltpu.make_async_copy(nat.at[pl.ds(f * share, share)], out.at[pl.ds(f * share, share)], sems.at[f])
        for f in range(FIELDS)
    ]
    for f in range(FIELDS):
        for yb in range(YB):

            def tile(kb, yb=yb, f=f):
                base = f * LEVELS + kb
                block = (yb * FIELDS + f) * KB + kb
                rows = end[pl.ds(pl.multiple_of(PAD + block * COLS, 8), COLS), :].T
                for yc in range(YC):
                    r = YB * yc + yb - HALO
                    if 0 <= r < ROWS:
                        for a in range(2):
                            at = pl.ds((base + a * 8 * KB) * ROWS + r, 8, stride=KB * ROWS)
                            nat[at, :] = rows[yc * KA + 8 * a : yc * KA + 8 * a + 8]

            unrolled(KB, TILES, tile)
        copies[f].start()

    target = lanes(COLS)
    block = 64
    for b in range(FIELDS * LEVELS // block):
        total = jnp.zeros((block, COLS), jnp.float32)
        for a in range(4):
            rows = []
            for c in range(block // 8):
                at = (b * block + c * 8) * ROWS + 4 * a
                part = [nat[pl.ds(at + i, 8, stride=ROWS), :] for i in range(4)]
                rows.append((part[0] + part[1]) + (part[2] + part[3]))
            gather = jnp.where(a * 32 + sublanes(COLS) // 4 == target, 1.0 / 16.0, 0.0).astype(jnp.float32)
            total = total + lax.dot_general(
                jnp.concatenate(rows, axis=0), gather, (((1,), (0,)), ((), ())),
                precision=HIGHEST, preferred_element_type=jnp.float32,
            )
        means[pl.ds(b * block, block), :] = total
    for copy in copies:
        copy.wait()


def feedback_kernel(sc, coarse, means, got1, got2, got3, blocks, out):
    me = sc[S_ME].astype(jnp.float32)
    for i in range(FIELDS * LEVELS // 8):
        rows = pl.ds(i * 8, 8)
        value = means[rows, :]
        for j, got in enumerate((got1, got2, got3)):
            value = jnp.where(blocks[pl.ds(j * 8, 8), :] == me, got[rows, :], value)
        old = coarse[rows, :]
        out[rows, :] = old + FEEDBACK * (value - old)


def call(kernel, outs, scratch, *args, far=(), far_out=(), cost=None):
    def spec(i, places, arg=None):
        if i in places:
            return pl.BlockSpec(memory_space=pltpu.HBM)
        small = arg is not None and arg.ndim == 1
        return pl.BlockSpec(memory_space=pltpu.SMEM if small else pltpu.VMEM)

    return pl.pallas_call(
        kernel,
        out_shape=[jax.ShapeDtypeStruct(s, jnp.float32) for s in outs],
        in_specs=[spec(i, far, a) for i, a in enumerate(args)],
        out_specs=[spec(i, far_out) for i in range(len(outs))],
        scratch_shapes=[pltpu.VMEM(s, jnp.float32) if isinstance(s, tuple) else s for s in scratch],
        cost_estimate=None if cost is None else pl.CostEstimate(flops=cost, bytes_accessed=cost, transcendentals=0),
        compiler_params=pltpu.CompilerParams(vmem_limit_bytes=VMEM_BYTES),
    )(*args)


def per_device(nest_state, mixing, land_mask, face_off, parent_state, parent_block, interp_idx, interp_w):
    tiles = lax.axis_size("nest")
    blocks = lax.axis_size("parent")
    n = lax.axis_index("nest")
    p = lax.axis_index("parent")
    x = n % GROUP
    own_block = parent_block[0, 0]

    def inside(code):
        return [(s, s ^ code) for s in range(tiles)]

    def across(pairs):
        links = []
        for g in range(tiles // GROUP):
            for a, b in pairs:
                i, j = GROUP * g + a, (GROUP * (g + 1) + b) % tiles
                links += [(i, j), (j, i)]
        return links

    rows_1 = [(s, s ^ 1) for s in range(blocks)]
    rows_2 = [(s, ((s + 1) ^ 1) - 1) if 0 < s < blocks - 1 else (s, blocks - 1 - s) for s in range(blocks)]
    links = [
        inside(1), inside(2), inside(3),
        across([(3, 0), (2, 1)]), across([(3, 1), (2, 0)]), across([(3, 2), (1, 0)]),
    ]
    x_even, low = x % 2 == 0, x < 2
    rel = [
        jnp.where(x_even, 1, -1),
        jnp.where(low, 2, -2),
        3 - 2 * x,
        jnp.where(low, -1 - 2 * x, 7 - 2 * x),
        jnp.where(low, -2, 2),
        jnp.where(x_even, -3, 3),
    ]
    sc = jnp.stack(
        [
            (p % 2 == 0).astype(jnp.int32),
            (p > 0).astype(jnp.int32),
            (p < blocks - 1).astype(jnp.int32),
            own_block ^ n,
        ]
        + [REACH + r for r in rel]
        + [x_even.astype(jnp.int32), low.astype(jnp.int32), own_block, n]
    ).astype(jnp.int32)

    nest2 = nest_state.reshape(FIELDS * LEVELS * ROWS, COLS)
    coarse = parent_state.reshape(FIELDS * LEVELS, COLS)
    natural = (FIELDS * LEVELS * ROWS, COLS)
    rows, narrow = (WIDE_ROWS, COLS), (ROWS, COLS)
    got = [lax.ppermute(coarse, "nest", links[i]) for i in range(3)]
    pay1, pay2 = call(rows_kernel, [rows, rows], [], sc, nest2)
    (ends,) = call(
        ends_kernel, [(YB * SHARE + 2 * ROWS, COLS)], [(2 * EXT, COLS)], nest2, land_mask, mixing, cost=SMALL
    )
    wide1 = lax.ppermute(pay1, "parent", rows_1)
    wide2 = lax.ppermute(pay2, "parent", rows_2)
    face, idx, weight = (
        face_off.T, interp_idx.transpose(1, 2, 0).reshape(8, ROWS), interp_w.transpose(1, 2, 0).reshape(8, ROWS)
    )
    coarse_rows = (FIELDS * LEVELS, COLS)
    table, offs, kept = call(
        table_kernel, [(2 * EXT, COLS), (2 * ROWS, COLS), coarse_rows],
        [(2 * EXT, COLS), coarse_rows, pltpu.VMEM((2, ROWS), jnp.int32), pltpu.VMEM((8, ROWS), jnp.int32),
         pltpu.VMEM((8, ROWS), jnp.float32), pltpu.SemaphoreType.DMA((4,))],
        coarse, face, idx, weight, far=(0, 1, 2, 3), cost=SMALL,
    )
    block, state_rows = (BLOCKS, COLS), (STATE_ROWS, COLS)
    og, swap = call(
        open_kernel, [(YB * SHARE, COLS), (SWAP_ROWS, COLS)], [coarse_rows], sc, kept, *got, table, offs, ends
    )
    edge1 = lax.ppermute(swap, "parent", rows_1)
    edge2 = lax.ppermute(swap, "parent", rows_2)
    ogx, offv, message = call(
        message_kernel, [(2 * BLOCKS, COLS), (8, COLS), (MESSAGE_ROWS, COLS)],
        [(2 * EXT, COLS), (YB * SHARE, COLS)], sc, og, offs, edge1, edge2,
    )
    nest_later, offv = lax.optimization_barrier((nest2, offv))
    state, coef = call(
        turn_kernel, [state_rows, (2 * YB * COLS, COLS)],
        [(2 * EXT, COLS), pltpu.VMEM(narrow, jnp.int32), pltpu.VMEM(narrow, jnp.float32), pltpu.SemaphoreType.DMA((2,))],
        sc, nest_later, wide1, wide2, edge1, edge2, land_mask, mixing, far=(6, 7),
    )
    first = [lax.ppermute(message, "nest", link) for link in links]
    work = [(SLOTS * SIDE_ROWS, COLS), state_rows] + [block] * 4
    state, edges = call(
        first_kernel, [state_rows, (4 * BLOCKS, COLS)], work, sc, state, message, ogx, coef, offv, *first
    )
    second = [lax.ppermute(edges, "nest", link) for link in links]
    new2, means, blocks = call(
        second_kernel, [natural, coarse_rows, (24, COLS)],
        work + [state_rows, natural, pltpu.SemaphoreType.DMA((FIELDS,))],
        sc, state, edges, ogx, coef, offv, *first, *second, far_out=(0,),
    )
    arrived = [lax.ppermute(means, "nest", links[i]) for i in range(3)]
    (parent_new,) = call(feedback_kernel, [coarse_rows], [], sc, kept, means, *arrived, blocks)
    return new2.reshape(nest_state.shape), parent_new.reshape(parent_state.shape)


def solution(mesh):
    return jax.shard_map(
        per_device,
        mesh=mesh,
        in_specs=(
            P(None, None, "parent", "nest"),
            P("parent", "nest"),
            P("parent", "nest"),
            P("parent", "nest"),
            P(None, None, "parent", "nest"),
            P("parent", "nest"),
            P("parent", "nest", None),
            P("parent", "nest", None),
        ),
        out_specs=(P(None, None, "parent", "nest"), P(None, None, "parent", "nest")),
        check_vma=False,
    )
```

```python
import jax
import jax.numpy as jnp
from jax import lax
from jax.experimental import pallas as pl
from jax.experimental.pallas import tpu as pltpu
from jax.sharding import PartitionSpec as P

FIELDS = 4
LEVELS = 64
ROWS = 16
COLS = 128
HALO = 4
EXT = ROWS + 2 * HALO
YB = 3
YC = 8
KB = 4
KA = 16
BLOCKS = YB * FIELDS * KB
PAD = 8
STATE_ROWS = BLOCKS * COLS + 2 * PAD
SIDE_ROWS = 4 * BLOCKS + 16
SHARE = 6 * 16 + 8
SWAP_ROWS = SHARE + 4 * ROWS
WIDE_ROWS = FIELDS * LEVELS * HALO
REACH = 3
SMALL = 1000
SLOTS = 2 * REACH + 1
GROUP = 4
VMEM_BYTES = 44 * 1024 * 1024

TIME_STEP = 0.1
TURN = 0.05
FEEDBACK = 0.5
HIGHEST = lax.Precision.HIGHEST

S_EVEN, S_TOP, S_BOTTOM, S_PBX, S_SLOT, S_XEVEN, S_LOW, S_PB, S_ME = 0, 1, 2, 3, 4, 10, 11, 12, 13


def lanes(rows=8):
    return lax.broadcasted_iota(jnp.int32, (rows, COLS), 1)


def sublanes(rows=8):
    return lax.broadcasted_iota(jnp.int32, (rows, COLS), 0)


def wide(row):
    return jnp.broadcast_to(row, (8, COLS))


def unrolled(count, step, body):
    def several(i, carry):
        for j in range(step):
            body(i * step + j)
        return carry

    lax.fori_loop(0, count // step, several, 0)


def rows_kernel(sc, nest, pay1, pay2):
    even = sc[S_EVEN] == 1
    first = jnp.where(even, ROWS - HALO, 0)
    second = jnp.where(even, 0, ROWS - HALO)

    def move(i):
        at, to = i * ROWS, i * HALO
        pay1[pl.ds(to, HALO), :] = nest[pl.ds(at + first, HALO), :]
        pay2[pl.ds(to, HALO), :] = nest[pl.ds(at + second, HALO), :]

    unrolled(FIELDS * LEVELS, 16, move)


def ends_kernel(nest, mask, mixing, ends, ext):
    nothing = jnp.zeros((8, COLS), jnp.float32)
    ext[...] = jnp.zeros_like(ext)
    planes = (mask[...].astype(jnp.float32), mixing[...])
    for i, plane in enumerate(planes):
        ext[pl.ds(i * EXT + HALO, ROWS), :] = plane
        ends[pl.ds(YB * SHARE + i * ROWS, ROWS), :] = plane
    for yb in range(YB):
        ends[pl.ds(yb * SHARE + 96, 8), :] = nothing
        for i in range(2):
            rows = [jnp.broadcast_to(ext[pl.ds(i * EXT + YB * yc + yb, 1), :], (KA, COLS)) for yc in range(YC)]
            tile = jnp.concatenate(rows, axis=0).T
            ends[pl.ds(yb * SHARE + 96 + i, 1), :] = tile[COLS - 1 : COLS]
            ends[pl.ds(yb * SHARE + 98 + i, 1), :] = tile[0:1]

        def take(i, yb=yb):
            base = (i // KB) * LEVELS + i % KB
            rows = []
            for yc in range(YC):
                r = YB * yc + yb - HALO
                for a in range(2):
                    if 0 <= r < ROWS:
                        rows.append(nest[pl.ds((base + a * 8 * KB) * ROWS + r, 8, stride=KB * ROWS), :])
                    else:
                        rows.append(nothing)
            tile = jnp.concatenate(rows, axis=0).T
            for c, x in enumerate((COLS - 1, 0, COLS - 2, 1)):
                ends[pl.ds(yb * SHARE + c * 16 + i, 1), :] = tile[x : x + 1]

        unrolled(16, TILES, take)


def table_kernel(coarse, face, idx, weight, table, offs, kept, spread, near, face_in, idx_in, weight_in, sems):
    pairs = ((coarse, near), (face, face_in), (idx, idx_in), (weight, weight_in))
    copies = [pltpu.make_async_copy(far, here, sems.at[i]) for i, (far, here) in enumerate(pairs)]
    for copy in copies:
        copy.start()
    for copy in copies:
        copy.wait()
    kept[...] = near[...]

    def upright(small):
        spread[pl.ds(0, 8), :] = jnp.zeros((8, COLS), jnp.float32)
        spread[pl.ds(0, small.shape[0]), 0:ROWS] = small.astype(jnp.float32)
        return spread[pl.ds(0, 8), :].T[:ROWS]

    face = upright(face_in[...])
    idx = upright(idx_in[...])
    weight = upright(weight_in[...])
    offs[pl.ds(0, ROWS), :] = jnp.broadcast_to(face[:, 0:1], (ROWS, COLS))
    offs[pl.ds(ROWS, ROWS), :] = jnp.broadcast_to(face[:, 1:2], (ROWS, COLS))
    cell = lanes(ROWS).astype(jnp.float32)
    spread[...] = jnp.zeros_like(spread)
    for side in range(2):
        total = jnp.zeros((ROWS, 1), jnp.float32)
        values = jnp.zeros((ROWS, COLS), jnp.float32)
        for j in range(4):
            c = side * 4 + j
            w = weight[:, c : c + 1]
            total = total + w
            values = values + jnp.where(idx[:, c : c + 1] == cell, w, 0.0)
        spread[pl.ds(side * EXT + HALO, ROWS), :] = values / total
    for side in range(2):
        for yb in range(YB):
            table[pl.ds(side * EXT + yb * YC, YC), :] = spread[pl.ds(side * EXT + yb, YC, stride=YB), :]


def open_kernel(sc, own, got1, got2, got3, table, offs, ends, og, swap, chosen):
    swap[pl.ds(SHARE, 2 * ROWS), :] = offs[...]
    swap[pl.ds(SHARE + 2 * ROWS, 2 * ROWS), :] = ends[pl.ds(YB * SHARE, 2 * ROWS), :]
    for yb in range(YB):
        og[pl.ds(yb * SHARE, 64), :] = ends[pl.ds(yb * SHARE, 64), :]
        og[pl.ds(yb * SHARE + 96, 8), :] = ends[pl.ds(yb * SHARE + 96, 8), :]
    pbx = sc[S_PBX]
    value = own[...]
    for code, got in ((1, got1), (2, got2), (3, got3)):
        value = jnp.where(pbx == code, got[...], value)
    chosen[...] = value
    rows = []
    for f in range(FIELDS):
        for kb in range(KB):
            for a in range(2):
                rows.append(chosen[pl.ds(f * LEVELS + kb + a * 8 * KB, 8, stride=KB), :])
    weights = jnp.concatenate([table[...], jnp.zeros((COLS - 2 * EXT, COLS), jnp.float32)], axis=0)
    values = lax.dot_general(
        jnp.concatenate(rows, axis=0), weights, (((1,), (1,)), ((), ())),
        precision=HIGHEST, preferred_element_type=jnp.float32,
    )
    shift = (lanes() // KA - sublanes()) % 8
    for half in range(2):
        upright = values[half * COLS : (half + 1) * COLS].T
        for i in range(2 * YB):
            part = upright[i * YC : (i + 1) * YC]
            value = part
            for d in range(1, 8):
                value = jnp.where(shift == d, pltpu.roll(pltpu.roll(part, KA * d, 1), 8 - d, 0), value)
            og[pl.ds((i % YB) * SHARE + 64 + (i // YB) * 16 + half * 8, 8), :] = value
    chunk = lanes(SHARE) // KA
    planes = [og[pl.ds(yb * SHARE, SHARE), :] for yb in range(YB)]
    swap[pl.ds(0, SHARE), :] = jnp.where(
        chunk % 4 == 3, pltpu.roll(planes[0], KA, 1),
        jnp.where(chunk % 4 == 0, pltpu.roll(planes[2], COLS - KA, 1), planes[1]),
    )


def columns_of(state, edges):
    for c, x in enumerate((COLS - 1, 0, COLS - 2, 1)):
        for i in range(BLOCKS // 8):
            edges[pl.ds(c * BLOCKS + 8 * i, 8), :] = state[pl.ds(PAD + 8 * i * COLS + x, 8, stride=COLS), :]


def halos(sc, one, two):
    even = sc[S_EVEN] == 1
    top = jnp.where(sc[S_TOP] == 1, jnp.where(even, two, one), 0.0)
    bottom = jnp.where(sc[S_BOTTOM] == 1, jnp.where(even, one, two), 0.0)
    return top, bottom


def turn_kernel(sc, nest, wide1, wide2, edge1, edge2, far_mask, far_mixing, state, coef, ext, mask, mixing, sems):
    copies = [
        pltpu.make_async_copy(far_mask, mask, sems.at[0]),
        pltpu.make_async_copy(far_mixing, mixing, sems.at[1]),
    ]
    for copy in copies:
        copy.start()
    pad = jnp.zeros((PAD, COLS), jnp.float32)
    state[pl.ds(0, PAD), :] = pad
    state[pl.ds(STATE_ROWS - PAD, PAD), :] = pad
    even = sc[S_EVEN] == 1
    top_in, bottom_in = sc[S_TOP] == 1, sc[S_BOTTOM] == 1
    for yb in range(YB):

        def tile(i, yb=yb):
            base = (i // KB) * LEVELS + i % KB
            rows = []
            for yc in range(YC):
                r = YB * yc + yb
                for a in range(2):
                    level = base + a * 8 * KB
                    if HALO <= r < HALO + ROWS:
                        rows.append(nest[pl.ds(level * ROWS + r - HALO, 8, stride=KB * ROWS), :])
                    else:
                        at = pl.ds(level * HALO + r % ROWS % HALO, 8, stride=KB * HALO)
                        one, two = wide1[at, :], wide2[at, :]
                        if r < HALO:
                            rows.append(jnp.where(top_in, jnp.where(even, two, one), 0.0))
                        else:
                            rows.append(jnp.where(bottom_in, jnp.where(even, one, two), 0.0))
            at = pl.multiple_of(PAD + (yb * 16 + i) * COLS, 8)
            state[pl.ds(at, COLS), :] = jnp.concatenate(rows, axis=0).T

        unrolled(16, TILES, tile)
    for copy in copies:
        copy.wait()
    for i, plane in enumerate((mask[...].astype(jnp.float32), mixing[...])):
        at = SHARE + (2 + i) * ROWS
        low, high = pl.ds(at, HALO), pl.ds(at + ROWS - HALO, HALO)
        top = halos(sc, edge1[high, :], edge2[high, :])[0]
        bottom = halos(sc, edge1[low, :], edge2[low, :])[1]
        ext[pl.ds(i * EXT, HALO), :] = top
        ext[pl.ds(i * EXT + HALO, ROWS), :] = plane
        ext[pl.ds(i * EXT + HALO + ROWS, HALO), :] = bottom
    for yb in range(YB):
        for i in range(2):
            rows = [
                jnp.broadcast_to(ext[pl.ds(i * EXT + YB * yc + yb, 1), :], (KA, COLS)) for yc in range(YC)
            ]
            coef[pl.ds((i * YB + yb) * COLS, COLS), :] = jnp.concatenate(rows, axis=0).T


def message_kernel(sc, og, offs, edge1, edge2, ogx, offv, edges, msg_e, msg_o, msg_lo, msg_hi, left, right, ext, joint):
    mine = sublanes() == lanes() // KA
    even = sc[S_EVEN] == 1
    for i in range(2):
        at = SHARE + i * ROWS
        one_low, one_high = edge1[pl.ds(at, HALO), :], edge1[pl.ds(at + ROWS - HALO, HALO), :]
        two_low, two_high = edge2[pl.ds(at, HALO), :], edge2[pl.ds(at + ROWS - HALO, HALO), :]
        ext[pl.ds(i * EXT, HALO), :] = jnp.where(even, two_high, one_high)
        ext[pl.ds(i * EXT + HALO, ROWS), :] = offs[pl.ds(i * ROWS, ROWS), :]
        ext[pl.ds(i * EXT + HALO + ROWS, HALO), :] = jnp.where(even, one_low, two_low)
        for yb in range(YB):
            away = ext[pl.ds(i * EXT + yb, YC, stride=YB), :]
            offv[pl.ds(i * YB + yb, 1), :] = jnp.sum(jnp.where(mine, away, 0.0), axis=0, keepdims=True)
    chunk = lanes(SHARE) // KA
    top, bottom = halos(sc, edge1[pl.ds(0, SHARE), :], edge2[pl.ds(0, SHARE), :])
    for yb in range(YB):
        rows = pl.ds(yb * SHARE, SHARE)
        row = YB * chunk + yb
        up = pltpu.roll(top, KA * (3, 4, 1)[yb], 1)
        down = pltpu.roll(bottom, KA * (7, 4, 5)[yb], 1)
        joint[rows, :] = jnp.where(row < HALO, up, jnp.where(row >= HALO + ROWS, down, og[rows, :]))
        for c in range(4):
            edges[pl.ds(c * BLOCKS + yb * 16, 16), :] = joint[pl.ds(yb * SHARE + c * 16, 16), :]
        for side in range(2):
            ogx[pl.ds(side * BLOCKS + yb * 16, 16), :] = joint[pl.ds(yb * SHARE + 64 + side * 16, 16), :]
    number = sc[S_PB].astype(jnp.float32)
    for ref, third, opened, fact, off in ((right, 2, 1, 0, 1), (left, 3, 0, 2, 0)):
        ref[pl.ds(0, 2 * BLOCKS), :] = edges[pl.ds(0, 2 * BLOCKS), :]
        ref[pl.ds(2 * BLOCKS, BLOCKS), :] = edges[pl.ds(third * BLOCKS, BLOCKS), :]
        ref[pl.ds(3 * BLOCKS, BLOCKS), :] = ogx[pl.ds(opened * BLOCKS, BLOCKS), :]
        ref[pl.ds(4 * BLOCKS, 16), :] = jnp.zeros((16, COLS), jnp.float32) + number
        for yb in range(YB):
            for i in range(2):
                ref[pl.ds(4 * BLOCKS + i * YB + yb, 1), :] = joint[pl.ds(yb * SHARE + 96 + fact + i, 1), :]
        ref[pl.ds(4 * BLOCKS + 2 * YB, YB), :] = offv[pl.ds(off * YB, YB), :]
    x_even, low = sc[S_XEVEN] == 1, sc[S_LOW] == 1
    msg_e[...] = jnp.where(x_even, right[...], left[...])
    msg_o[...] = jnp.where(x_even, left[...], right[...])
    msg_lo[...] = jnp.where(low, right[...], left[...])
    msg_hi[...] = jnp.where(low, left[...], right[...])


def coefficients(wet, mix):
    kmix = wet * mix
    return kmix, wet - 4.0 * TIME_STEP * wet - 2.0 * kmix, TIME_STEP * wet, TURN * wet


def advance_edge(q, east, west, wet, mix):
    sub, lane = sublanes(), lanes() % KA
    new = []
    for yb in range(YB):
        kmix, centre, base, turn = coefficients(wide(wet[yb]), wide(mix[yb]))
        flow = q[yb][1]
        swapped = pltpu.roll(flow, 4, 0)
        cu = turn * jnp.where(sub < 4, flow, swapped)
        cv = turn * jnp.where(sub < 4, swapped, flow)
        pair = []
        for half in range(2):
            c = q[yb][half]
            above = jnp.where(
                sub % KB >= 1, pltpu.roll(c, 1, 0),
                jnp.where(lane == 0, c, pltpu.roll(pltpu.roll(c, 5, 0), 1, 1)),
            )
            below = jnp.where(
                sub % KB < KB - 1, pltpu.roll(c, 7, 0),
                jnp.where(lane == KA - 1, c, pltpu.roll(pltpu.roll(c, 3, 0), COLS - 1, 1)),
            )
            south = q[yb - 1][half] if yb > 0 else pltpu.roll(q[YB - 1][half], KA, 1)
            north = q[yb + 1][half] if yb < YB - 1 else pltpu.roll(q[0][half], COLS - KA, 1)
            value = (centre * c + (base - cu) * east[yb][half]) + ((base + cu) * west[yb][half] + (base - cv) * north)
            value = value + ((base + cv) * south + kmix * (above + below))
            if half == 1:
                value = value + jnp.where(sub < 4, cv, -cu)
            pair.append(value)
        new.append(pair)
    return new


def ghosts(side, ogx, offv, west0, east0, west1, east1):
    def column(slot, c):
        return [
            [side[pl.ds(slot * SIDE_ROWS + c * BLOCKS + yb * 16 + half * 8, 8), :] for half in range(2)]
            for yb in range(YB)
        ]

    def fact(slot, i):
        return [side[pl.ds(slot * SIDE_ROWS + 4 * BLOCKS + i * YB + yb, 1), :] for yb in range(YB)]

    def pick(away, choices, value):
        for e, choice in choices:
            value = [
                [jnp.where(wide(away[yb]) == e, choice[yb][half], value[yb][half]) for half in range(2)]
                for yb in range(YB)
            ]
        return value

    def put(ref, value):
        for yb in range(YB):
            for half in range(2):
                ref[pl.ds(yb * 16 + half * 8, 8), :] = value[yb][half]

    for sign, first, second in ((-1, west0, west1), (1, east0, east1)):
        which = 0 if sign < 0 else 1
        away = [offv[pl.ds(which * YB + yb, 1), :] for yb in range(YB)]
        opened = [
            [ogx[pl.ds(which * BLOCKS + yb * 16 + half * 8, 8), :] for half in range(2)] for yb in range(YB)
        ]
        reach = range(1, REACH + 1)
        put(first, pick(away, [(d, column(REACH + sign * d, which)) for d in reach], opened))
        later = opened
        for d in reach:
            slot = REACH + sign * d
            outer = pick(
                fact(slot, 2), [(e, column(slot - sign * e, 1 - which)) for e in reach], column(slot, 3)
            )
            inner = column(slot, 2)
            east, west = (outer, inner) if sign < 0 else (inner, outer)
            new = advance_edge(column(slot, which), east, west, fact(slot, 0), fact(slot, 1))
            later = pick(away, [(d, new)], later)
        put(second, later)


def substep(src, dst, west_ghost, east_ghost, coef):
    sub, ka = sublanes(), lanes() % KA

    def block(yb, f, kb):
        return (yb * FIELDS + f) * KB + kb

    for yb in range(YB):

        def group(xg, first, last, yb=yb):
            x = xg * 8

            def load(yb, f, kb, shift=0):
                return src[pl.ds(PAD + block(yb, f, kb) * COLS + x + shift, 8), :]

            kmix, centre, base, turn = coefficients(
                coef[pl.ds(yb * COLS + x, 8), :], coef[pl.ds((YB + yb) * COLS + x, 8), :]
            )
            q = [[load(yb, f, kb) for kb in range(KB)] for f in range(FIELDS)]
            for kb in range(KB):
                cu, cv = turn * q[2][kb], turn * q[3][kb]
                ke, kw, kn, ks = base - cu, base + cu, base - cv, base + cv
                for f in range(FIELDS):
                    c = q[f][kb]
                    b = block(yb, f, kb)
                    west, east = load(yb, f, kb, -1), load(yb, f, kb, 1)
                    if first:
                        west = jnp.where(sub == 0, wide(west_ghost[pl.ds(b, 1), :]), west)
                    if last:
                        east = jnp.where(sub == 7, wide(east_ghost[pl.ds(b, 1), :]), east)
                    south = load(yb - 1, f, kb) if yb > 0 else pltpu.roll(load(YB - 1, f, kb), KA, 1)
                    north = load(yb + 1, f, kb) if yb < YB - 1 else pltpu.roll(load(0, f, kb), COLS - KA, 1)
                    above = q[f][kb - 1] if kb > 0 else jnp.where(ka == 0, c, pltpu.roll(q[f][KB - 1], 1, 1))
                    below = q[f][kb + 1] if kb < KB - 1 else jnp.where(ka == KA - 1, c, pltpu.roll(q[f][0], COLS - 1, 1))
                    new = (centre * c + ke * east) + (kw * west + kn * north)
                    new = new + (ks * south + kmix * (above + below))
                    if f == 2:
                        new = new + cv
                    if f == 3:
                        new = new - cu
                    dst[pl.ds(PAD + b * COLS + x, 8), :] = new

        group(0, True, False)

        def body(i, carry, group=group):
            for j in range(UNROLL):
                group(1 + i * UNROLL + j, False, False)
            return carry

        lax.fori_loop(0, (COLS // 8 - 2) // UNROLL, body, 0)
        group(COLS // 8 - 1, False, True)


UNROLL = 7
TILES = 4


def clear_pads(*refs):
    for ref in refs:
        ref[pl.ds(0, PAD), :] = jnp.zeros((PAD, COLS), jnp.float32)
        ref[pl.ds(STATE_ROWS - PAD, PAD), :] = jnp.zeros((PAD, COLS), jnp.float32)


def first_kernel(
    sc, state, own, ogx, coef, offv, r0, r1, r2, r3, r4, r5, out, edges, side, mid, west0, east0, west1, east1
):
    clear_pads(mid, out)
    side[pl.ds(REACH * SIDE_ROWS, 2 * BLOCKS), :] = own[pl.ds(0, 2 * BLOCKS), :]
    for j, r in enumerate((r0, r1, r2, r3, r4, r5)):
        side[pl.ds(pl.multiple_of(sc[S_SLOT + j] * SIDE_ROWS, 8), SIDE_ROWS), :] = r[...]
    ghosts(side, ogx, offv, west0, east0, west1, east1)
    substep(state, mid, west0, east0, coef)
    substep(mid, out, west1, east1, coef)
    columns_of(out, edges)


def second_kernel(
    sc, state, own, ogx, coef, offv, r0, r1, r2, r3, r4, r5, s0, s1, s2, s3, s4, s5,
    out, means, blocks, side, mid, west0, east0, west1, east1, end, nat, sems,
):
    clear_pads(mid)
    side[pl.ds(REACH * SIDE_ROWS, 2 * BLOCKS), :] = own[pl.ds(0, 2 * BLOCKS), :]
    for j, (r, s) in enumerate(zip((r0, r1, r2, r3, r4, r5), (s0, s1, s2, s3, s4, s5))):
        slot = sc[S_SLOT + j]
        at = slot * SIDE_ROWS
        third = pl.multiple_of(jnp.where(slot > REACH, 3 * BLOCKS, 2 * BLOCKS), 8)
        side[pl.ds(pl.multiple_of(at, 8), 2 * BLOCKS), :] = s[pl.ds(0, 2 * BLOCKS), :]
        side[pl.ds(pl.multiple_of(at + 2 * BLOCKS, 8), BLOCKS), :] = s[pl.ds(third, BLOCKS), :]
        side[pl.ds(pl.multiple_of(at + 3 * BLOCKS, 8), BLOCKS + 16), :] = r[pl.ds(3 * BLOCKS, BLOCKS + 16), :]
    ghosts(side, ogx, offv, west0, east0, west1, east1)
    substep(state, mid, west0, east0, coef)
    substep(mid, end, west1, east1, coef)
    for j in range(3):
        blocks[pl.ds(j * 8, 8), :] = wide((r0, r1, r2)[j][pl.ds(SIDE_ROWS - 1, 1), :])
    share = LEVELS * ROWS
    copies = [
        pltpu.make_async_copy(nat.at[pl.ds(f * share, share)], out.at[pl.ds(f * share, share)], sems.at[f])
        for f in range(FIELDS)
    ]
    for f in range(FIELDS):
        for yb in range(YB):

            def tile(kb, yb=yb, f=f):
                base = f * LEVELS + kb
                block = (yb * FIELDS + f) * KB + kb
                rows = end[pl.ds(pl.multiple_of(PAD + block * COLS, 8), COLS), :].T
                for yc in range(YC):
                    r = YB * yc + yb - HALO
                    if 0 <= r < ROWS:
                        for a in range(2):
                            at = pl.ds((base + a * 8 * KB) * ROWS + r, 8, stride=KB * ROWS)
                            nat[at, :] = rows[yc * KA + 8 * a : yc * KA + 8 * a + 8]

            unrolled(KB, TILES, tile)
        copies[f].start()

    target = lanes(COLS)
    block = 64
    for b in range(FIELDS * LEVELS // block):
        total = jnp.zeros((block, COLS), jnp.float32)
        for a in range(4):
            rows = []
            for c in range(block // 8):
                at = (b * block + c * 8) * ROWS + 4 * a
                part = [nat[pl.ds(at + i, 8, stride=ROWS), :] for i in range(4)]
                rows.append((part[0] + part[1]) + (part[2] + part[3]))
            gather = jnp.where(a * 32 + sublanes(COLS) // 4 == target, 1.0 / 16.0, 0.0).astype(jnp.float32)
            total = total + lax.dot_general(
                jnp.concatenate(rows, axis=0), gather, (((1,), (0,)), ((), ())),
                precision=HIGHEST, preferred_element_type=jnp.float32,
            )
        means[pl.ds(b * block, block), :] = total
    for copy in copies:
        copy.wait()


def feedback_kernel(sc, coarse, means, got1, got2, got3, blocks, out):
    me = sc[S_ME].astype(jnp.float32)
    for i in range(FIELDS * LEVELS // 8):
        rows = pl.ds(i * 8, 8)
        value = means[rows, :]
        for j, got in enumerate((got1, got2, got3)):
            value = jnp.where(blocks[pl.ds(j * 8, 8), :] == me, got[rows, :], value)
        old = coarse[rows, :]
        out[rows, :] = old + FEEDBACK * (value - old)


def call(kernel, outs, scratch, *args, far=(), far_out=(), cost=None):
    def spec(i, places, arg=None):
        if i in places:
            return pl.BlockSpec(memory_space=pltpu.HBM)
        small = arg is not None and arg.ndim == 1
        return pl.BlockSpec(memory_space=pltpu.SMEM if small else pltpu.VMEM)

    return pl.pallas_call(
        kernel,
        out_shape=[jax.ShapeDtypeStruct(s, jnp.float32) for s in outs],
        in_specs=[spec(i, far, a) for i, a in enumerate(args)],
        out_specs=[spec(i, far_out) for i in range(len(outs))],
        scratch_shapes=[pltpu.VMEM(s, jnp.float32) if isinstance(s, tuple) else s for s in scratch],
        cost_estimate=None if cost is None else pl.CostEstimate(flops=cost, bytes_accessed=cost, transcendentals=0),
        compiler_params=pltpu.CompilerParams(vmem_limit_bytes=VMEM_BYTES),
    )(*args)


def per_device(nest_state, mixing, land_mask, face_off, parent_state, parent_block, interp_idx, interp_w):
    tiles = lax.axis_size("nest")
    blocks = lax.axis_size("parent")
    n = lax.axis_index("nest")
    p = lax.axis_index("parent")
    x = n % GROUP
    own_block = parent_block[0, 0]

    def inside(code):
        return [(s, s ^ code) for s in range(tiles)]

    def across(pairs):
        links = []
        for g in range(tiles // GROUP):
            for a, b in pairs:
                i, j = GROUP * g + a, (GROUP * (g + 1) + b) % tiles
                links += [(i, j), (j, i)]
        return links

    rows_1 = [(s, s ^ 1) for s in range(blocks)]
    rows_2 = [(s, ((s + 1) ^ 1) - 1) if 0 < s < blocks - 1 else (s, blocks - 1 - s) for s in range(blocks)]
    links = [
        inside(1), inside(2), inside(3),
        across([(3, 0), (2, 1)]), across([(3, 1), (2, 0)]), across([(3, 2), (1, 0)]),
    ]
    x_even, low = x % 2 == 0, x < 2
    rel = [
        jnp.where(x_even, 1, -1),
        jnp.where(low, 2, -2),
        3 - 2 * x,
        jnp.where(low, -1 - 2 * x, 7 - 2 * x),
        jnp.where(low, -2, 2),
        jnp.where(x_even, -3, 3),
    ]
    sc = jnp.stack(
        [
            (p % 2 == 0).astype(jnp.int32),
            (p > 0).astype(jnp.int32),
            (p < blocks - 1).astype(jnp.int32),
            own_block ^ n,
        ]
        + [REACH + r for r in rel]
        + [x_even.astype(jnp.int32), low.astype(jnp.int32), own_block, n]
    ).astype(jnp.int32)

    nest2 = nest_state.reshape(FIELDS * LEVELS * ROWS, COLS)
    coarse = parent_state.reshape(FIELDS * LEVELS, COLS)
    natural = (FIELDS * LEVELS * ROWS, COLS)
    rows, narrow = (WIDE_ROWS, COLS), (ROWS, COLS)
    got = [lax.ppermute(coarse, "nest", links[i]) for i in range(3)]
    pay1, pay2 = call(rows_kernel, [rows, rows], [], sc, nest2)
    (ends,) = call(
        ends_kernel, [(YB * SHARE + 2 * ROWS, COLS)], [(2 * EXT, COLS)], nest2, land_mask, mixing, cost=SMALL
    )
    wide1 = lax.ppermute(pay1, "parent", rows_1)
    wide2 = lax.ppermute(pay2, "parent", rows_2)
    face, idx, weight = (
        face_off.T, interp_idx.transpose(1, 2, 0).reshape(8, ROWS), interp_w.transpose(1, 2, 0).reshape(8, ROWS)
    )
    coarse_rows = (FIELDS * LEVELS, COLS)
    table, offs, kept = call(
        table_kernel, [(2 * EXT, COLS), (2 * ROWS, COLS), coarse_rows],
        [(2 * EXT, COLS), coarse_rows, pltpu.VMEM((2, ROWS), jnp.int32), pltpu.VMEM((8, ROWS), jnp.int32),
         pltpu.VMEM((8, ROWS), jnp.float32), pltpu.SemaphoreType.DMA((4,))],
        coarse, face, idx, weight, far=(0, 1, 2, 3), cost=SMALL,
    )
    block, state_rows = (BLOCKS, COLS), (STATE_ROWS, COLS)
    og, swap = call(
        open_kernel, [(YB * SHARE, COLS), (SWAP_ROWS, COLS)], [coarse_rows], sc, kept, *got, table, offs, ends
    )
    edge1 = lax.ppermute(swap, "parent", rows_1)
    edge2 = lax.ppermute(swap, "parent", rows_2)
    side = (SIDE_ROWS, COLS)
    ogx, offv, edges, msg_e, msg_o, msg_lo, msg_hi = call(
        message_kernel, [(2 * BLOCKS, COLS), (8, COLS), (4 * BLOCKS, COLS)] + [side] * 4,
        [side, side, (2 * EXT, COLS), (YB * SHARE, COLS)], sc, og, offs, edge1, edge2,
    )
    nest_later, offv = lax.optimization_barrier((nest2, offv))
    state, coef = call(
        turn_kernel, [state_rows, (2 * YB * COLS, COLS)],
        [(2 * EXT, COLS), pltpu.VMEM(narrow, jnp.int32), pltpu.VMEM(narrow, jnp.float32), pltpu.SemaphoreType.DMA((2,))],
        sc, nest_later, wide1, wide2, edge1, edge2, land_mask, mixing, far=(6, 7),
    )
    msgs = [msg_e, msg_lo, msg_lo, msg_hi, msg_hi, msg_o]
    first = [lax.ppermute(m, "nest", link) for m, link in zip(msgs, links)]
    work = [(SLOTS * SIDE_ROWS, COLS), state_rows] + [block] * 4
    state, edges = call(
        first_kernel, [state_rows, (4 * BLOCKS, COLS)], work, sc, state, edges, ogx, coef, offv, *first
    )
    second = [lax.ppermute(edges, "nest", link) for link in links]
    new2, means, blocks = call(
        second_kernel, [natural, coarse_rows, (24, COLS)],
        work + [state_rows, natural, pltpu.SemaphoreType.DMA((FIELDS,))],
        sc, state, edges, ogx, coef, offv, *first, *second, far_out=(0,),
    )
    arrived = [lax.ppermute(means, "nest", links[i]) for i in range(3)]
    (parent_new,) = call(feedback_kernel, [coarse_rows], [], sc, kept, means, *arrived, blocks)
    return new2.reshape(nest_state.shape), parent_new.reshape(parent_state.shape)


def solution(mesh):
    return jax.shard_map(
        per_device,
        mesh=mesh,
        in_specs=(
            P(None, None, "parent", "nest"),
            P("parent", "nest"),
            P("parent", "nest"),
            P("parent", "nest"),
            P(None, None, "parent", "nest"),
            P("parent", "nest"),
            P("parent", "nest", None),
            P("parent", "nest", None),
        ),
        out_specs=(P(None, None, "parent", "nest"), P(None, None, "parent", "nest")),
        check_vma=False,
    )
```
